512 devices in a mesh: rcv: 64 (over z_hi, y, core), shot: 8 (over x, z_lo).
Axes of the slice: x: 4, y: 8, z: 8 (z_hi: 4, z_lo: 2; z = z_hi * 2 + z_lo), core: 2. Of those that a mesh axis runs over, the one named last changes fastest.
Arguments:
- records: bfloat16 [2, 8, 1024, 8192], P(None, 'shot', None, 'rcv')
- live_mask: int32 [8, 8192], P('shot', 'rcv'), may hold values 0 or 1
- owners: int32 [3], replicated, may hold values from 0 to 63, as said below
Outputs:
- gathers: float32 [3, 128, 8, 8192], P(None, 'shot', None, 'rcv')
The draws below stay inside these ranges and needn't reach their ends.
Inputs may be any that keep to these rules, and one draw needn't show every extreme that they name: `owners`: 3 different indices; the first and the last rcv index are always among them, in a drawn order.
All inputs are finite; a program needn't handle non-finite values. No bound on the sum of `live_mask` on one device may be relied on, other than what follows from the above.
Results may differ from the reference program's by a relative error of at most 0.004.
Values may be sent and summed in bfloat16 or wider, within the bound.
A program may use at most 64 MiB of HBM per device.

```python
import math
import jax
import jax.numpy as jnp
from jax import lax

CHAN = 128
FREQ = 1024
BLOCKS = 3
LAGS = 8
STRIDE = 16
SHOTS = 8
RCV_ALL = 8192
N_RCV = 64


def draw_records(key, part):
    key = jax.random.fold_in(key, 11)
    keys = jax.random.split(key, 3)
    spectrum = jnp.exp(jax.random.uniform(keys[2], (1, 1, FREQ, 1), jnp.float32, math.log(0.5), math.log(5.0)))
    base = jax.random.normal(keys[0], (2, SHOTS, FREQ, RCV_ALL), jnp.float32)
    scales = jnp.exp(jax.random.uniform(keys[1], (1, SHOTS, 1, RCV_ALL), jnp.float32, 0.0, math.log(10.0)))
    return (base * scales * spectrum).astype(jnp.bfloat16)


def draw_owners(key, part):
    key = jax.random.fold_in(key, 23)
    keys = jax.random.split(key, 2)
    middle = jax.random.permutation(keys[0], N_RCV - 2)[:BLOCKS - 2].astype(jnp.int32) + 1
    ends = jnp.array([0, N_RCV - 1], dtype=jnp.int32)
    chosen = jnp.concatenate([ends, middle])
    return jax.random.permutation(keys[1], chosen).astype(jnp.int32)


def touch_ends(values, stream_key, smallest, top_value):
    dims = values.shape
    index_at = [jax.random.randint(jax.random.fold_in(stream_key, axis), (), 0, dims[axis]) for axis in range(len(dims))]
    values = values.at[tuple(index_at)].set(smallest)
    longest = dims.index(max(dims))
    index_at[longest] = (index_at[longest] + 1) % dims[longest]
    return values.at[tuple(index_at)].set(top_value)


def setup_inputs(seed: int = 0) -> dict:
    seeds = jax.random.split(jax.random.key(seed), 4)
    records = draw_records(jax.random.fold_in(seeds[3], 71), 0)
    live_mask = touch_ends((jax.random.randint(seeds[1], (SHOTS, RCV_ALL), 0, 8) < 7).astype(jnp.int32), jax.random.fold_in(seeds[1], 1), 0, 1)
    owners = draw_owners(jax.random.fold_in(seeds[3], 71), 0)
    return dict(records=records, live_mask=live_mask, owners=owners)


def lag_tables(total_shots):
    freq_index = jnp.arange(FREQ, dtype=jnp.float32)
    lag_index = jnp.arange(LAGS, dtype=jnp.float32)
    shifts = (lag_index - float(LAGS // 2)) * float(STRIDE) + float(STRIDE // 2)
    lag_taper = 0.54 + 0.46 * jnp.cos(2.0 * math.pi * (lag_index + 0.5) / LAGS - math.pi)
    phases = math.pi * freq_index[:, None] * shifts[None, :] / FREQ
    weights = lag_taper[None, :] / jnp.sqrt(jnp.float32(total_shots * FREQ))
    return (jnp.cos(phases) * weights, jnp.sin(phases) * weights)

def whiten(traces, live_mask):
    values = traces.astype(jnp.float32)
    power = lax.optimization_barrier(jnp.mean(values * values, axis=(0, 2), keepdims=True))
    live = live_mask.astype(jnp.float32)[None, :, None, :]
    return values * live / jnp.sqrt(power + 1e-06)

def steer_lags(whitened, cos_table, sin_table):
    real_part = whitened[0][:, :, None, :]
    imag_part = whitened[1][:, :, None, :]
    cos_part = cos_table[None, :, :, None]
    sin_part = sin_table[None, :, :, None]
    first = real_part * cos_part - imag_part * sin_part
    second = real_part * sin_part + imag_part * cos_part
    return jnp.stack([first, second]).astype(jnp.bfloat16)

def reference(records, live_mask, owners):
    cos_table, sin_table = lag_tables(SHOTS)
    panels = []
    for block in range(BLOCKS):
        start = (owners[block] * CHAN).astype(jnp.int32)
        traces = lax.dynamic_slice_in_dim(records, start, CHAN, 3)
        masks = lax.dynamic_slice_in_dim(live_mask, start, CHAN, 1)
        panels.append(whiten(traces, masks).astype(jnp.bfloat16))
    panels = jnp.stack(panels).astype(jnp.float32)

    def receiver_block(index):
        start = (index * CHAN).astype(jnp.int32)
        traces = lax.dynamic_slice_in_dim(records, start, CHAN, 3)
        masks = lax.dynamic_slice_in_dim(live_mask, start, CHAN, 1)
        steered = steer_lags(whiten(traces, masks), cos_table, sin_table).astype(jnp.float32)
        return jnp.einsum('bcsfv,csflr->bvlr', panels, steered)
    results = lax.map(receiver_block, jnp.arange(N_RCV, dtype=jnp.int32))
    results = jnp.transpose(results, (1, 2, 3, 0, 4))
    return results.reshape(BLOCKS, CHAN, LAGS, N_RCV * CHAN)
```

```python
import functools
import math

import jax
import jax.numpy as jnp
import numpy as np
from jax import lax
from jax.experimental import pallas as pl
from jax.experimental.pallas import tpu as pltpu
from jax.sharding import PartitionSpec as P

FREQ = 1024
CHAN = 128
BLOCKS = 3
LAGS = 8
STRIDE = 16
N_ZH = 4
N_Y = 8
CHIPS = N_ZH * N_Y
N_RCV = 2 * CHIPS
SHOTS = 8
PIECE = FREQ // CHIPS
GROUP = FREQ // N_Y
ROWS = CHAN // SHOTS
WIDE = LAGS * CHAN
MESH = pl.DeviceIdType.MESH


def lag_tables():
    f32 = np.float32
    freq_index = np.arange(FREQ, dtype=f32)
    lag_index = np.arange(LAGS, dtype=f32)
    shifts = (lag_index - f32(LAGS // 2)) * f32(STRIDE) + f32(STRIDE // 2)
    taper = f32(0.54) + f32(0.46) * np.cos(f32(2.0 * math.pi) * (lag_index + f32(0.5)) / f32(LAGS) - f32(math.pi))
    phases = f32(math.pi) * freq_index[:, None] * shifts[None, :] / f32(FREQ)
    weights = taper[None, :] / np.sqrt(f32(SHOTS * FREQ))
    half = LAGS // 2
    cos_table = (np.cos(phases) * weights)[:, :half]
    sin_table = (np.sin(phases) * weights)[:, :half]
    return np.concatenate([cos_table, sin_table], axis=1).astype(f32)


def kernel(
    owners_ref, mask_ref, tab_ref, rec_hbm, out_ref,
    rec, own, xb, ms, mr, pb, st, part, rb,
    load_sem, sib_s, sib_r, scat_s, scat_r, mid_s, mid_r,
    z_s, z_r, y_s, y_r, d_s, d_r, rs_s, rs_r,
):
    r = lax.axis_index("rcv")
    s = lax.axis_index("shot")
    q = lax.div(r, 2)
    core = lax.rem(r, 2)
    zh = lax.div(q, N_Y)
    y = lax.rem(q, N_Y)
    sib = r + 1 - 2 * core

    def chip(d):
        return lax.rem(q + d, CHIPS)

    def shot(d):
        return lax.rem(s + d, SHOTS)

    barrier = pltpu.get_barrier_semaphore()

    def greet(d, carry):
        pl.semaphore_signal(barrier, inc=1, device_id={"rcv": chip(d) * 2 + core}, device_id_type=MESH)
        return carry

    pl.semaphore_signal(barrier, inc=1, device_id={"rcv": sib}, device_id_type=MESH)
    load = pltpu.make_async_copy(rec_hbm, rec, load_sem)
    load.start()
    lax.fori_loop(1, CHIPS, greet, 0)

    def greet_shot(d, carry):
        pl.semaphore_signal(barrier, inc=1, device_id={"shot": shot(d)}, device_id_type=MESH)
        return carry

    lax.fori_loop(1, SHOTS, greet_shot, 0)

    load.wait()

    def add_power(i, acc):
        rows = pl.ds(pl.multiple_of(i * 64, 64), 64)
        for p in range(2):
            v = rec[p, rows, :].astype(jnp.float32)
            v = v * v
            for j in range(8):
                acc = acc + v[8 * j:8 * j + 8]
        return acc

    total = lax.fori_loop(0, FREQ // 64, add_power, jnp.zeros((8, CHAN), jnp.float32))
    power = jnp.sum(total, axis=0, keepdims=True) * (1.0 / (2 * FREQ))
    gain = mask_ref[...].astype(jnp.float32) / jnp.sqrt(power + 1e-06)

    def whiten_part(p):
        def body(i, carry):
            rows = pl.ds(pl.multiple_of(i * 128, 128), 128)
            own[p, rows, :] = (rec[p, rows, :].astype(jnp.float32) * gain).astype(jnp.bfloat16)
            return carry
        lax.fori_loop(0, FREQ // 128, body, 0)

    whiten_part(1 - core)
    pl.semaphore_wait(barrier, CHIPS - 1 + 1 + SHOTS - 1)
    swap = pltpu.make_async_remote_copy(
        src_ref=own.at[1 - core], dst_ref=xb, send_sem=sib_s, recv_sem=sib_r,
        device_id={"rcv": sib}, device_id_type=MESH)
    swap.start()
    whiten_part(core)
    swap.wait_recv()

    mid = owners_ref[0] + owners_ref[1] + owners_ref[2] - (N_RCV - 1)
    is_me = jnp.where(mid == r, 1.0, 0.0).astype(jnp.float32)
    is_sib = jnp.where(mid == sib, 1.0, 0.0).astype(jnp.float32)

    def pick(i, carry):
        rows = pl.ds(pl.multiple_of(i * 128, 128), 128)
        mine = own[core, rows, :].astype(jnp.float32) * is_me
        other = xb[rows, :].astype(jnp.float32) * is_sib
        ms[rows, :] = (mine + other).astype(jnp.bfloat16)
        return carry

    lax.fori_loop(0, FREQ // 128, pick, 0)

    def piece_row(q2):
        z2 = lax.div(q2, N_Y)
        y2 = lax.rem(q2, N_Y)
        return pl.multiple_of(y2 * GROUP + z2 * PIECE, PIECE)

    my_row = piece_row(q)
    base = core * FREQ

    def rows_of(start, size):
        return pl.ds(pl.multiple_of(start, PIECE), size)

    def send_mid(d, carry):
        q2 = chip(d)
        pltpu.make_async_remote_copy(
            src_ref=ms.at[rows_of(piece_row(q2), PIECE), :],
            dst_ref=mr.at[rows_of((d - 1) * PIECE, PIECE), :],
            send_sem=mid_s, recv_sem=mid_r,
            device_id={"rcv": q2 * 2 + core}, device_id_type=MESH).start()
        return carry

    lax.fori_loop(1, CHIPS, send_mid, 0)

    def scatter(blk, src):
        def body(d, carry):
            q2 = chip(d)
            row = piece_row(q2)
            pltpu.make_async_remote_copy(
                src_ref=src.at[rows_of(row, PIECE), :],
                dst_ref=pb.at[blk, rows_of(base + row, PIECE), :],
                send_sem=scat_s.at[blk], recv_sem=scat_r.at[blk],
                device_id={"rcv": q2 * 2 + core}, device_id_type=MESH).start()
            return carry
        lax.fori_loop(1, CHIPS, body, 0)
        pb[blk, rows_of(base + my_row, PIECE), :] = src[rows_of(my_row, PIECE), :]

    @pl.when(r == 0)
    def _():
        scatter(0, own.at[0])

    @pl.when(r == 1)
    def _():
        scatter(0, xb)

    @pl.when(r == N_RCV - 1)
    def _():
        scatter(1, own.at[1])

    @pl.when(r == N_RCV - 2)
    def _():
        scatter(1, xb)

    half = LAGS // 2

    def steer(i, carry):
        rows = pl.ds(pl.multiple_of(i * 16, 16), 16)
        low = pl.ds(pl.multiple_of(FREQ + i * 16, 16), 16)
        a = rec[0, rows, :].astype(jnp.float32) * gain
        b = rec[1, rows, :].astype(jnp.float32) * gain
        for l in range(half):
            c = jnp.broadcast_to(tab_ref[rows, l:l + 1], (16, CHAN))
            t = jnp.broadcast_to(tab_ref[rows, half + l:half + l + 1], (16, CHAN))
            ac, bt, at, bc = a * c, b * t, a * t, b * c
            near = slice(l * CHAN, (l + 1) * CHAN)
            far = slice((LAGS - 1 - l) * CHAN, (LAGS - l) * CHAN)
            st[rows, near] = (ac - bt).astype(jnp.bfloat16)
            st[rows, far] = (ac + bt).astype(jnp.bfloat16)
            st[low, near] = (at + bc).astype(jnp.bfloat16)
            st[low, far] = (bc - at).astype(jnp.bfloat16)
        return carry

    lax.fori_loop(0, FREQ // 16, steer, 0)

    def wait_rows(ref, sem):
        pltpu.make_async_copy(ref, ref, sem).wait()

    def column_copy(blk, d):
        z2 = lax.rem(zh + d, N_ZH)
        rows = rows_of(base + my_row, PIECE)
        return pltpu.make_async_remote_copy(
            src_ref=pb.at[blk, rows, :], dst_ref=pb.at[blk, rows, :],
            send_sem=z_s.at[blk, d - 1], recv_sem=z_r.at[blk, d - 1],
            device_id={"rcv": (z2 * N_Y + y) * 2 + core}, device_id_type=MESH)

    def column_send(blk):
        for d in range(1, N_ZH):
            column_copy(blk, d).start()

    def column_recv(blk):
        for d in range(1, N_ZH):
            column_copy(blk, d).wait_recv()

    def ring_rows(k, way):
        yp = lax.rem(y + (k - 1 if way else N_Y - k + 1), N_Y)
        if k < N_Y // 2:
            return rows_of(base + yp * GROUP, GROUP)
        return rows_of(base + yp * GROUP + way * (GROUP // 2), GROUP // 2)

    def ring_copy(blk, k, way):
        y2 = lax.rem(y + (N_Y - 1 if way else 1), N_Y)
        rows = ring_rows(k, way)
        return pltpu.make_async_remote_copy(
            src_ref=pb.at[blk, rows, :], dst_ref=pb.at[blk, rows, :],
            send_sem=y_s.at[blk, way, k - 1], recv_sem=y_r.at[blk, way, k - 1],
            device_id={"rcv": (zh * N_Y + y2) * 2 + core}, device_id_type=MESH)

    def to_sibling(blk, rows):
        pltpu.make_async_remote_copy(
            src_ref=pb.at[blk, rows, :], dst_ref=pb.at[blk, rows, :],
            send_sem=d_s.at[blk], recv_sem=d_r.at[blk],
            device_id={"rcv": sib}, device_id_type=MESH).start()

    def ring_send(blk, k):
        for way in range(2):
            ring_copy(blk, k, way).start()

    def ring_step(blk, k):
        for way in range(2):
            ring_copy(blk, k, way).wait_recv()
            if k < N_Y // 2:
                ring_copy(blk, k + 1, way).start()
        for way in range(2):
            yp = lax.rem(y + (k if way else N_Y - k), N_Y)
            if k < N_Y // 2:
                to_sibling(blk, rows_of(base + yp * GROUP, GROUP))
            else:
                to_sibling(blk, rows_of(base + yp * GROUP + way * (GROUP // 2), GROUP // 2))

    def ring_start(blk):
        column_recv(blk)
        ring_send(blk, 1)
        to_sibling(blk, rows_of(base + y * GROUP, GROUP))

    def correlate(blk):
        wait_rows(pb.at[blk, pl.ds(0, FREQ), :], d_r.at[blk])
        for n in range(4):
            cols = slice(n * 256, (n + 1) * 256)
            part[blk, :, cols] = lax.dot_general(
                pb[blk], st[:, cols], (((0,), (0,)), ((), ())),
                preferred_element_type=jnp.float32).astype(jnp.bfloat16)

        def body(d, carry):
            s2 = shot(d)
            pltpu.make_async_remote_copy(
                src_ref=part.at[blk, pl.ds(pl.multiple_of(s2 * ROWS, ROWS), ROWS), :],
                dst_ref=rb.at[blk, pl.ds(pl.multiple_of((d - 1) * ROWS, ROWS), ROWS), :],
                send_sem=rs_s.at[blk], recv_sem=rs_r.at[blk],
                device_id={"shot": s2}, device_id_type=MESH).start()
            return carry

        lax.fori_loop(1, SHOTS, body, 0)

    def stack(blk):
        wait_rows(rb.at[blk], rs_r.at[blk])
        mine = pl.ds(pl.multiple_of(s * ROWS, ROWS), ROWS)
        for l in range(LAGS):
            cols = slice(l * CHAN, (l + 1) * CHAN)
            acc = part[blk, mine, cols].astype(jnp.float32)
            for d in range(SHOTS - 1):
                acc = acc + rb[blk, d * ROWS:(d + 1) * ROWS, cols].astype(jnp.float32)
            out_ref[blk, :, l, :] = acc

    for blk, root in ((0, 0), (1, CHIPS - 1)):
        @pl.when(q != root)
        def _():
            wait_rows(pb.at[blk, rows_of(base + my_row, PIECE), :], scat_r.at[blk])
        column_send(blk)

    wait_rows(mr, mid_r)
    acc = ms[rows_of(my_row, PIECE), :]
    for d in range(CHIPS - 1):
        acc = acc + mr[d * PIECE:(d + 1) * PIECE, :]
    pb[2, rows_of(base + my_row, PIECE), :] = acc
    column_send(2)

    ring_start(0)
    ring_start(1)
    for k in (1, 2):
        ring_step(0, k)
        ring_step(1, k)
    ring_start(2)
    ring_step(0, 3)
    ring_step(1, 3)
    ring_step(2, 1)
    ring_step(0, 4)
    ring_step(1, 4)
    ring_step(2, 2)
    correlate(0)
    ring_step(2, 3)
    correlate(1)
    ring_step(2, 4)
    correlate(2)
    for blk in range(BLOCKS):
        stack(blk)

    swap.wait_send()
    wait_rows(mr, mid_s)
    for blk, root in ((0, 0), (1, CHIPS - 1)):
        @pl.when(q == root)
        def _():
            wait_rows(mr, scat_s.at[blk])
    for blk in range(BLOCKS):
        for d in range(1, N_ZH):
            column_copy(blk, d).wait_send()
        for k in range(1, N_Y // 2 + 1):
            for way in range(2):
                ring_copy(blk, k, way).wait_send()
        wait_rows(pb.at[blk, pl.ds(0, FREQ), :], d_s.at[blk])
        wait_rows(rb.at[blk], rs_s.at[blk])


def on_device(records, live_mask, owners):
    bf16, f32 = jnp.bfloat16, jnp.float32
    dma = pltpu.SemaphoreType.DMA
    stacked = pl.pallas_call(
        kernel,
        out_shape=jax.ShapeDtypeStruct((BLOCKS, ROWS, LAGS, CHAN), f32),
        in_specs=[
            pl.BlockSpec(memory_space=pltpu.SMEM),
            pl.BlockSpec(memory_space=pltpu.VMEM),
            pl.BlockSpec(memory_space=pltpu.VMEM),
            pl.BlockSpec(memory_space=pl.ANY),
        ],
        out_specs=pl.BlockSpec(memory_space=pltpu.VMEM),
        scratch_shapes=[
            pltpu.VMEM((2, FREQ, CHAN), bf16),
            pltpu.VMEM((2, FREQ, CHAN), bf16),
            pltpu.VMEM((FREQ, CHAN), bf16),
            pltpu.VMEM((FREQ, CHAN), bf16),
            pltpu.VMEM(((CHIPS - 1) * PIECE, CHAN), bf16),
            pltpu.VMEM((BLOCKS, 2 * FREQ, CHAN), bf16),
            pltpu.VMEM((2 * FREQ, WIDE), bf16),
            pltpu.VMEM((BLOCKS, CHAN, WIDE), bf16),
            pltpu.VMEM((BLOCKS, (SHOTS - 1) * ROWS, WIDE), bf16),
            dma, dma, dma, dma((2,)), dma((2,)), dma, dma,
            dma((BLOCKS, N_ZH - 1)), dma((BLOCKS, N_ZH - 1)),
            dma((BLOCKS, 2, N_Y // 2)), dma((BLOCKS, 2, N_Y // 2)),
            dma((BLOCKS,)), dma((BLOCKS,)), dma((BLOCKS,)), dma((BLOCKS,)),
        ],
        cost_estimate=pl.CostEstimate(flops=1_700_000_000, bytes_accessed=1_500_000, transcendentals=0),
        compiler_params=pltpu.CompilerParams(
            collective_id=0, has_side_effects=True, vmem_limit_bytes=40 * 2**20),
    )(owners, live_mask, jnp.asarray(lag_tables()), records.reshape(2, FREQ, CHAN))
    first = (owners == 0)[:, None, None, None]
    last = (owners == N_RCV - 1)[:, None, None, None]
    return jnp.where(first, stacked[0:1], jnp.where(last, stacked[1:2], stacked[2:3]))


def solution(mesh):
    in_specs = (P(None, "shot", None, "rcv"), P("shot", "rcv"), P())
    out_specs = P(None, "shot", None, "rcv")
    return jax.shard_map(
        on_device, mesh=mesh, in_specs=in_specs, out_specs=out_specs, check_vma=False
    )
```

```python
import functools
import math

import jax
import jax.numpy as jnp
import numpy as np
from jax import lax
from jax.experimental import pallas as pl
from jax.experimental.pallas import tpu as pltpu
from jax.sharding import PartitionSpec as P

FREQ = 1024
CHAN = 128
BLOCKS = 3
LAGS = 8
STRIDE = 16
N_ZH = 4
N_Y = 8
CHIPS = N_ZH * N_Y
N_RCV = 2 * CHIPS
SHOTS = 8
PIECE = FREQ // CHIPS
GROUP = FREQ // N_Y
ROWS = CHAN // SHOTS
WIDE = LAGS * CHAN
MESH = pl.DeviceIdType.MESH


def lag_tables():
    f32 = np.float32
    freq_index = np.arange(FREQ, dtype=f32)
    lag_index = np.arange(LAGS, dtype=f32)
    shifts = (lag_index - f32(LAGS // 2)) * f32(STRIDE) + f32(STRIDE // 2)
    taper = f32(0.54) + f32(0.46) * np.cos(f32(2.0 * math.pi) * (lag_index + f32(0.5)) / f32(LAGS) - f32(math.pi))
    phases = f32(math.pi) * freq_index[:, None] * shifts[None, :] / f32(FREQ)
    weights = taper[None, :] / np.sqrt(f32(SHOTS * FREQ))
    half = LAGS // 2
    cos_table = (np.cos(phases) * weights)[:, :half]
    sin_table = (np.sin(phases) * weights)[:, :half]
    return np.concatenate([cos_table, sin_table], axis=1).astype(f32)


def kernel(
    owners_ref, mask_hbm, tab_hbm, rec_hbm, out_ref,
    mask_ref, tab_ref, rec, own, xb, ms, mr, pb, st, part, rb, res,
    mask_sem, tab_sem, load_sem, sib_s, sib_r, scat_s, scat_r, mid_s, mid_r,
    z_s, z_r, y_s, y_r, d_s, d_r, rs_s, rs_r,
):
    r = lax.axis_index("rcv")
    s = lax.axis_index("shot")
    q = lax.div(r, 2)
    core = lax.rem(r, 2)
    zh = lax.div(q, N_Y)
    y = lax.rem(q, N_Y)
    sib = r + 1 - 2 * core

    def chip(d):
        return lax.rem(q + d, CHIPS)

    def shot(d):
        return lax.rem(s + d, SHOTS)

    barrier = pltpu.get_barrier_semaphore()

    def greet(d, carry):
        pl.semaphore_signal(barrier, inc=1, device_id={"rcv": chip(d) * 2 + core}, device_id_type=MESH)
        return carry

    pl.semaphore_signal(barrier, inc=1, device_id={"rcv": sib}, device_id_type=MESH)
    load = pltpu.make_async_copy(rec_hbm, rec, load_sem)
    load.start()
    load_mask = pltpu.make_async_copy(mask_hbm, mask_ref, mask_sem)
    load_mask.start()
    load_tab = pltpu.make_async_copy(tab_hbm, tab_ref, tab_sem)
    load_tab.start()
    lax.fori_loop(1, CHIPS, greet, 0)

    def greet_shot(d, carry):
        pl.semaphore_signal(barrier, inc=1, device_id={"shot": shot(d)}, device_id_type=MESH)
        return carry

    lax.fori_loop(1, SHOTS, greet_shot, 0)

    load.wait()

    def add_power(i, acc):
        rows = pl.ds(pl.multiple_of(i * 64, 64), 64)
        for p in range(2):
            v = rec[p, rows, :].astype(jnp.float32)
            v = v * v
            for j in range(8):
                acc = acc + v[8 * j:8 * j + 8]
        return acc

    total = lax.fori_loop(0, FREQ // 64, add_power, jnp.zeros((8, CHAN), jnp.float32))
    power = jnp.sum(total, axis=0, keepdims=True) * (1.0 / (2 * FREQ))
    load_mask.wait()
    gain = mask_ref[...].astype(jnp.float32) / jnp.sqrt(power + 1e-06)

    def whiten_part(p):
        def body(i, carry):
            rows = pl.ds(pl.multiple_of(i * 128, 128), 128)
            own[p, rows, :] = (rec[p, rows, :].astype(jnp.float32) * gain).astype(jnp.bfloat16)
            return carry
        lax.fori_loop(0, FREQ // 128, body, 0)

    whiten_part(1 - core)
    pl.semaphore_wait(barrier, CHIPS - 1 + 1 + SHOTS - 1)
    swap = pltpu.make_async_remote_copy(
        src_ref=own.at[1 - core], dst_ref=xb, send_sem=sib_s, recv_sem=sib_r,
        device_id={"rcv": sib}, device_id_type=MESH)
    swap.start()
    whiten_part(core)
    swap.wait_recv()

    mid = owners_ref[0] + owners_ref[1] + owners_ref[2] - (N_RCV - 1)
    is_me = jnp.where(mid == r, 1.0, 0.0).astype(jnp.float32)
    is_sib = jnp.where(mid == sib, 1.0, 0.0).astype(jnp.float32)

    def pick(i, carry):
        rows = pl.ds(pl.multiple_of(i * 128, 128), 128)
        mine = own[core, rows, :].astype(jnp.float32) * is_me
        other = xb[rows, :].astype(jnp.float32) * is_sib
        ms[rows, :] = (mine + other).astype(jnp.bfloat16)
        return carry

    lax.fori_loop(0, FREQ // 128, pick, 0)

    def piece_row(q2):
        z2 = lax.div(q2, N_Y)
        y2 = lax.rem(q2, N_Y)
        return pl.multiple_of(y2 * GROUP + z2 * PIECE, PIECE)

    my_row = piece_row(q)
    base = core * FREQ

    def rows_of(start, size):
        return pl.ds(pl.multiple_of(start, PIECE), size)

    def send_mid(d, carry):
        q2 = chip(d)
        pltpu.make_async_remote_copy(
            src_ref=ms.at[rows_of(piece_row(q2), PIECE), :],
            dst_ref=mr.at[rows_of((d - 1) * PIECE, PIECE), :],
            send_sem=mid_s, recv_sem=mid_r,
            device_id={"rcv": q2 * 2 + core}, device_id_type=MESH).start()
        return carry

    lax.fori_loop(1, CHIPS, send_mid, 0)

    def scatter(blk, src):
        def body(d, carry):
            q2 = chip(d)
            row = piece_row(q2)
            pltpu.make_async_remote_copy(
                src_ref=src.at[rows_of(row, PIECE), :],
                dst_ref=pb.at[blk, rows_of(base + row, PIECE), :],
                send_sem=scat_s.at[blk], recv_sem=scat_r.at[blk],
                device_id={"rcv": q2 * 2 + core}, device_id_type=MESH).start()
            return carry
        lax.fori_loop(1, CHIPS, body, 0)
        pb[blk, rows_of(base + my_row, PIECE), :] = src[rows_of(my_row, PIECE), :]

    @pl.when(r == 0)
    def _():
        scatter(0, own.at[0])

    @pl.when(r == 1)
    def _():
        scatter(0, xb)

    @pl.when(r == N_RCV - 1)
    def _():
        scatter(1, own.at[1])

    @pl.when(r == N_RCV - 2)
    def _():
        scatter(1, xb)

    half = LAGS // 2

    def steer(i, carry):
        rows = pl.ds(pl.multiple_of(i * 16, 16), 16)
        low = pl.ds(pl.multiple_of(FREQ + i * 16, 16), 16)
        a = rec[0, rows, :].astype(jnp.float32) * gain
        b = rec[1, rows, :].astype(jnp.float32) * gain
        for l in range(half):
            c = jnp.broadcast_to(tab_ref[rows, l:l + 1], (16, CHAN))
            t = jnp.broadcast_to(tab_ref[rows, half + l:half + l + 1], (16, CHAN))
            ac, bt, at, bc = a * c, b * t, a * t, b * c
            near = slice(l * CHAN, (l + 1) * CHAN)
            far = slice((LAGS - 1 - l) * CHAN, (LAGS - l) * CHAN)
            st[rows, near] = (ac - bt).astype(jnp.bfloat16)
            st[rows, far] = (ac + bt).astype(jnp.bfloat16)
            st[low, near] = (at + bc).astype(jnp.bfloat16)
            st[low, far] = (bc - at).astype(jnp.bfloat16)
        return carry

    load_tab.wait()
    lax.fori_loop(0, FREQ // 16, steer, 0)

    def wait_rows(ref, sem):
        pltpu.make_async_copy(ref, ref, sem).wait()

    def column_copy(blk, d):
        z2 = lax.rem(zh + d, N_ZH)
        rows = rows_of(base + my_row, PIECE)
        return pltpu.make_async_remote_copy(
            src_ref=pb.at[blk, rows, :], dst_ref=pb.at[blk, rows, :],
            send_sem=z_s.at[blk, d - 1], recv_sem=z_r.at[blk, d - 1],
            device_id={"rcv": (z2 * N_Y + y) * 2 + core}, device_id_type=MESH)

    def column_send(blk):
        for d in range(1, N_ZH):
            column_copy(blk, d).start()

    def column_recv(blk):
        for d in range(1, N_ZH):
            column_copy(blk, d).wait_recv()

    def ring_at(offset):
        return lax.rem(y + N_Y + offset, N_Y)

    def ring_rows(offset, way, whole):
        start = base + ring_at(offset) * GROUP
        if whole:
            return rows_of(start, GROUP)
        return rows_of(start + way * (GROUP // 2), GROUP // 2)

    def ring_copy(blk, way, j):
        sign = -1 if way else 1
        rows = ring_rows(0 if j < 2 else -2 * sign, way, j < 3)
        y2 = ring_at((2, 1, 1, 2)[j] * sign)
        return pltpu.make_async_remote_copy(
            src_ref=pb.at[blk, rows, :], dst_ref=pb.at[blk, rows, :],
            send_sem=y_s.at[blk, way, j], recv_sem=y_r.at[blk, way, j],
            device_id={"rcv": (zh * N_Y + y2) * 2 + core}, device_id_type=MESH)

    def to_sibling(blk, rows):
        pltpu.make_async_remote_copy(
            src_ref=pb.at[blk, rows, :], dst_ref=pb.at[blk, rows, :],
            send_sem=d_s.at[blk], recv_sem=d_r.at[blk],
            device_id={"rcv": sib}, device_id_type=MESH).start()

    def ring_recv(blk, j):
        for way in range(2):
            sign = -1 if way else 1
            ring_copy(blk, way, j).wait_recv()
            if j == 0:
                ring_copy(blk, way, 2).start()
                ring_copy(blk, way, 3).start()
            to_sibling(blk, ring_rows(-(2, 1, 3, 4)[j] * sign, way, j < 3))

    def ring_start(blk):
        column_recv(blk)
        for j in range(2):
            for way in range(2):
                ring_copy(blk, way, j).start()
        to_sibling(blk, ring_rows(0, 0, True))

    def correlate(blk):
        wait_rows(pb.at[blk, pl.ds(0, FREQ), :], d_r.at[blk])
        for n in range(4):
            cols = slice(n * 256, (n + 1) * 256)
            part[blk, :, cols] = lax.dot_general(
                pb[blk], st[:, cols], (((0,), (0,)), ((), ())),
                preferred_element_type=jnp.float32).astype(jnp.bfloat16)

        def body(d, carry):
            s2 = shot(d)
            pltpu.make_async_remote_copy(
                src_ref=part.at[blk, pl.ds(pl.multiple_of(s2 * ROWS, ROWS), ROWS), :],
                dst_ref=rb.at[blk, pl.ds(pl.multiple_of((d - 1) * ROWS, ROWS), ROWS), :],
                send_sem=rs_s.at[blk], recv_sem=rs_r.at[blk],
                device_id={"shot": s2}, device_id_type=MESH).start()
            return carry

        lax.fori_loop(1, SHOTS, body, 0)

    def stack(blk):
        wait_rows(rb.at[blk], rs_r.at[blk])
        mine = pl.ds(pl.multiple_of(s * ROWS, ROWS), ROWS)
        for l in range(LAGS):
            cols = slice(l * CHAN, (l + 1) * CHAN)
            acc = part[blk, mine, cols].astype(jnp.float32)
            for d in range(SHOTS - 1):
                acc = acc + rb[blk, d * ROWS:(d + 1) * ROWS, cols].astype(jnp.float32)
            res[blk, :, l, :] = acc

    for blk, root in ((0, 0), (1, CHIPS - 1)):
        @pl.when(q != root)
        def _():
            wait_rows(pb.at[blk, rows_of(base + my_row, PIECE), :], scat_r.at[blk])
        column_send(blk)

    wait_rows(mr, mid_r)
    acc = ms[rows_of(my_row, PIECE), :]
    for d in range(CHIPS - 1):
        acc = acc + mr[d * PIECE:(d + 1) * PIECE, :]
    pb[2, rows_of(base + my_row, PIECE), :] = acc
    column_send(2)

    for blk in range(BLOCKS):
        ring_start(blk)
    for blk in range(BLOCKS):
        ring_recv(blk, 0)
    for blk in range(BLOCKS):
        for j in range(1, 4):
            ring_recv(blk, j)
        correlate(blk)
    for blk in range(BLOCKS):
        stack(blk)

    for b in range(BLOCKS):
        owner = jnp.full((ROWS, LAGS, CHAN), owners_ref[b], jnp.int32)
        out_ref[b] = jnp.where(owner == 0, res[0], jnp.where(owner == N_RCV - 1, res[1], res[2]))

    swap.wait_send()
    wait_rows(mr, mid_s)
    for blk, root in ((0, 0), (1, CHIPS - 1)):
        @pl.when(q == root)
        def _():
            wait_rows(mr, scat_s.at[blk])
    for blk in range(BLOCKS):
        for d in range(1, N_ZH):
            column_copy(blk, d).wait_send()
        for j in range(4):
            for way in range(2):
                ring_copy(blk, way, j).wait_send()
        wait_rows(pb.at[blk, pl.ds(0, FREQ), :], d_s.at[blk])
        wait_rows(rb.at[blk], rs_s.at[blk])


def on_device(records, live_mask, owners):
    bf16, f32 = jnp.bfloat16, jnp.float32
    dma = pltpu.SemaphoreType.DMA
    return pl.pallas_call(
        kernel,
        out_shape=jax.ShapeDtypeStruct((BLOCKS, ROWS, LAGS, CHAN), f32),
        in_specs=[
            pl.BlockSpec(memory_space=pltpu.SMEM),
            pl.BlockSpec(memory_space=pltpu.HBM),
            pl.BlockSpec(memory_space=pltpu.HBM),
            pl.BlockSpec(memory_space=pltpu.HBM),
        ],
        out_specs=pl.BlockSpec(memory_space=pltpu.VMEM),
        scratch_shapes=[
            pltpu.VMEM((1, CHAN), jnp.int32),
            pltpu.VMEM((FREQ, LAGS), f32),
            pltpu.VMEM((2, FREQ, CHAN), bf16),
            pltpu.VMEM((2, FREQ, CHAN), bf16),
            pltpu.VMEM((FREQ, CHAN), bf16),
            pltpu.VMEM((FREQ, CHAN), bf16),
            pltpu.VMEM(((CHIPS - 1) * PIECE, CHAN), bf16),
            pltpu.VMEM((BLOCKS, 2 * FREQ, CHAN), bf16),
            pltpu.VMEM((2 * FREQ, WIDE), bf16),
            pltpu.VMEM((BLOCKS, CHAN, WIDE), bf16),
            pltpu.VMEM((BLOCKS, (SHOTS - 1) * ROWS, WIDE), bf16),
            pltpu.VMEM((BLOCKS, ROWS, LAGS, CHAN), f32),
            dma, dma, dma, dma, dma, dma((2,)), dma((2,)), dma, dma,
            dma((BLOCKS, N_ZH - 1)), dma((BLOCKS, N_ZH - 1)),
            dma((BLOCKS, 2, 4)), dma((BLOCKS, 2, 4)),
            dma((BLOCKS,)), dma((BLOCKS,)), dma((BLOCKS,)), dma((BLOCKS,)),
        ],
        cost_estimate=pl.CostEstimate(flops=1_700_000_000, bytes_accessed=1_500_000, transcendentals=0),
        compiler_params=pltpu.CompilerParams(
            collective_id=0, has_side_effects=True, vmem_limit_bytes=64 * 2**20),
    )(owners, live_mask, jnp.asarray(lag_tables()), records.reshape(2, FREQ, CHAN))


def solution(mesh):
    in_specs = (P(None, "shot", None, "rcv"), P("shot", "rcv"), P())
    out_specs = P(None, "shot", None, "rcv")
    return jax.shard_map(
        on_device, mesh=mesh, in_specs=in_specs, out_specs=out_specs, check_vma=False
    )
```

```python
import functools
import math

import jax
import jax.numpy as jnp
import numpy as np
from jax import lax
from jax.experimental import pallas as pl
from jax.experimental.pallas import tpu as pltpu
from jax.sharding import PartitionSpec as P

FREQ = 1024
CHAN = 128
BLOCKS = 3
LAGS = 8
STRIDE = 16
N_ZH = 4
N_Y = 8
CHIPS = N_ZH * N_Y
N_RCV = 2 * CHIPS
SHOTS = 8
GROUP = FREQ // N_Y
HALF = GROUP // 2
ROWS = CHAN // SHOTS
WIDE = LAGS * CHAN
SPAN = WIDE // 2
MESH = pl.DeviceIdType.MESH


def lag_tables():
    f32 = np.float32
    freq_index = np.arange(FREQ, dtype=f32)
    lag_index = np.arange(LAGS, dtype=f32)
    shifts = (lag_index - f32(LAGS // 2)) * f32(STRIDE) + f32(STRIDE // 2)
    taper = f32(0.54) + f32(0.46) * np.cos(f32(2.0 * math.pi) * (lag_index + f32(0.5)) / f32(LAGS) - f32(math.pi))
    phases = f32(math.pi) * freq_index[:, None] * shifts[None, :] / f32(FREQ)
    weights = taper[None, :] / np.sqrt(f32(SHOTS * FREQ))
    half = LAGS // 2
    cos_table = (np.cos(phases) * weights)[:, :half]
    sin_table = (np.sin(phases) * weights)[:, :half]
    return np.concatenate([cos_table, sin_table], axis=1).astype(f32)


def kernel(
    owners_ref, mask_hbm, tab_hbm, rec_hbm, out_ref,
    mask_ref, tab_ref, rec, own, xb, ms, mr, mp, mz, pb, st, part, rb, res,
    mask_sem, tab_sem, load_sem, sib_s, sib_r, scat_s, scat_r, mid_s, mid_r,
    mz_s, mz_r, z_s, z_r, y_s, y_r, d_s, d_r, rs_s, rs_r,
):
    r = lax.axis_index("rcv")
    s = lax.axis_index("shot")
    q = lax.div(r, 2)
    core = lax.rem(r, 2)
    zh = lax.div(q, N_Y)
    y = lax.rem(q, N_Y)
    sib = r + 1 - 2 * core

    def row_dev(d):
        return (zh * N_Y + lax.rem(y + d + N_Y, N_Y)) * 2 + core

    def column_dev(d):
        return (lax.rem(zh + d, N_ZH) * N_Y + y) * 2 + core

    def shot(d):
        return lax.rem(s + d, SHOTS)

    barrier = pltpu.get_barrier_semaphore()

    def greet(dev):
        pl.semaphore_signal(barrier, inc=1, device_id=dev, device_id_type=MESH)

    load = pltpu.make_async_copy(rec_hbm, rec, load_sem)
    load.start()
    load_mask = pltpu.make_async_copy(mask_hbm, mask_ref, mask_sem)
    load_mask.start()
    load_tab = pltpu.make_async_copy(tab_hbm, tab_ref, tab_sem)
    load_tab.start()
    for d in range(N_Y - 1, 0, -1):
        greet({"rcv": row_dev(d)})
    for d in range(1, N_ZH):
        greet({"rcv": column_dev(d)})
    greet({"rcv": sib})
    for d in range(1, SHOTS):
        greet({"shot": shot(d)})

    load.wait()

    def add_power(i, acc):
        rows = pl.ds(pl.multiple_of(i * 64, 64), 64)
        for p in range(2):
            v = rec[p, rows, :].astype(jnp.float32)
            v = v * v
            for j in range(8):
                acc = acc + v[8 * j:8 * j + 8]
        return acc

    total = lax.fori_loop(0, FREQ // 64, add_power, jnp.zeros((8, CHAN), jnp.float32))
    power = jnp.sum(total, axis=0, keepdims=True) * (1.0 / (2 * FREQ))
    load_mask.wait()
    gain = mask_ref[...].astype(jnp.float32) / jnp.sqrt(power + 1e-06)

    def whiten_part(p):
        def body(i, carry):
            rows = pl.ds(pl.multiple_of(i * 128, 128), 128)
            own[p, rows, :] = (rec[p, rows, :].astype(jnp.float32) * gain).astype(jnp.bfloat16)
            return carry
        lax.fori_loop(0, FREQ // 128, body, 0)

    whiten_part(1 - core)
    pl.semaphore_wait(barrier, N_Y - 1 + N_ZH - 1 + 1 + SHOTS - 1)
    swap = pltpu.make_async_remote_copy(
        src_ref=own.at[1 - core], dst_ref=xb, send_sem=sib_s, recv_sem=sib_r,
        device_id={"rcv": sib}, device_id_type=MESH)
    swap.start()
    whiten_part(core)
    swap.wait_recv()

    base = core * FREQ

    def rows_of(start, size):
        return pl.ds(pl.multiple_of(start, 16), size)

    my_rows = rows_of(base + y * GROUP, GROUP)

    def scatter(blk, src):
        for d in range(1, N_Y):
            row = lax.rem(y + d, N_Y) * GROUP
            pltpu.make_async_remote_copy(
                src_ref=src.at[rows_of(row, GROUP), :],
                dst_ref=pb.at[blk, rows_of(base + row, GROUP), :],
                send_sem=scat_s.at[blk], recv_sem=scat_r.at[blk],
                device_id={"rcv": row_dev(d)}, device_id_type=MESH).start()
        pb[blk, my_rows, :] = src[rows_of(y * GROUP, GROUP), :]

    @pl.when(r == 0)
    def _():
        scatter(0, own.at[0])

    @pl.when(r == 1)
    def _():
        scatter(0, xb)

    @pl.when(r == N_RCV - 1)
    def _():
        scatter(1, own.at[1])

    @pl.when(r == N_RCV - 2)
    def _():
        scatter(1, xb)

    mid = owners_ref[0] + owners_ref[1] + owners_ref[2] - (N_RCV - 1)
    is_me = jnp.where(mid == r, 1.0, 0.0).astype(jnp.float32)
    is_sib = jnp.where(mid == sib, 1.0, 0.0).astype(jnp.float32)

    def pick(i, carry):
        rows = pl.ds(pl.multiple_of(i * 128, 128), 128)
        mine = own[core, rows, :].astype(jnp.float32) * is_me
        other = xb[rows, :].astype(jnp.float32) * is_sib
        ms[rows, :] = (mine + other).astype(jnp.bfloat16)
        return carry

    lax.fori_loop(0, FREQ // 128, pick, 0)

    for h in range(2):
        for d in (4, 3, 5, 2, 6, 1, 7):
            pltpu.make_async_remote_copy(
                src_ref=ms.at[rows_of(lax.rem(y + d, N_Y) * GROUP + h * HALF, HALF), :],
                dst_ref=mr.at[h, (d - 1) * HALF:d * HALF, :],
                send_sem=mid_s.at[h], recv_sem=mid_r.at[h],
                device_id={"rcv": row_dev(d)}, device_id_type=MESH).start()

    half = LAGS // 2

    def steer(i, carry):
        rows = pl.ds(pl.multiple_of(i * 16, 16), 16)
        low = pl.ds(pl.multiple_of(FREQ + i * 16, 16), 16)
        a = rec[0, rows, :].astype(jnp.float32) * gain
        b = rec[1, rows, :].astype(jnp.float32) * gain
        for l in range(half):
            c = jnp.broadcast_to(tab_ref[rows, l:l + 1], (16, CHAN))
            t = jnp.broadcast_to(tab_ref[rows, half + l:half + l + 1], (16, CHAN))
            ac, bt, at, bc = a * c, b * t, a * t, b * c
            near = slice(l * CHAN, (l + 1) * CHAN)
            far = slice((LAGS - 1 - l) * CHAN, (LAGS - l) * CHAN)
            st[rows, near] = (ac - bt).astype(jnp.bfloat16)
            st[rows, far] = (ac + bt).astype(jnp.bfloat16)
            st[low, near] = (at + bc).astype(jnp.bfloat16)
            st[low, far] = (bc - at).astype(jnp.bfloat16)
        return carry

    load_tab.wait()
    lax.fori_loop(0, FREQ // 16, steer, 0)

    def wait_rows(ref, sem):
        pltpu.make_async_copy(ref, ref, sem).wait()

    def column_send(blk):
        for d in range(1, N_ZH):
            pltpu.make_async_remote_copy(
                src_ref=pb.at[blk, my_rows, :], dst_ref=pb.at[blk, my_rows, :],
                send_sem=z_s.at[blk], recv_sem=z_r.at[blk],
                device_id={"rcv": column_dev(d)}, device_id_type=MESH).start()

    def mid_copy(h, d):
        return pltpu.make_async_remote_copy(
            src_ref=mp.at[h], dst_ref=mz.at[h, d - 1],
            send_sem=mz_s.at[h, d - 1], recv_sem=mz_r.at[h, d - 1],
            device_id={"rcv": column_dev(d)}, device_id_type=MESH)

    def mid_row(h):
        wait_rows(mr.at[h], mid_r.at[h])
        acc = ms[rows_of(y * GROUP + h * HALF, HALF), :]
        for d in range(N_Y - 1):
            acc = acc + mr[h, d * HALF:(d + 1) * HALF, :]
        mp[h] = acc
        for d in (2, 1, 3):
            mid_copy(h, d).start()

    def mid_column(h):
        acc = mp[h]
        for d in range(1, N_ZH):
            mid_copy(h, d).wait_recv()
            acc = acc + mz[h, d - 1]
        pb[2, rows_of(base + y * GROUP + h * HALF, HALF), :] = acc

    def ring_at(offset):
        return lax.rem(y + N_Y + offset, N_Y)

    def ring_rows(part_set, offset, way, j):
        _, low, size, _ = part_set
        start = base + ring_at(offset) * GROUP + low
        if j < 3:
            return rows_of(start, size)
        return rows_of(start + way * (size // 2), size // 2)

    def ring_copy(part_set, way, j):
        blk, _, _, at = part_set
        sign = -1 if way else 1
        rows = ring_rows(part_set, 0 if j < 2 else -2 * sign, way, j)
        return pltpu.make_async_remote_copy(
            src_ref=pb.at[blk, rows, :], dst_ref=pb.at[blk, rows, :],
            send_sem=y_s.at[at, way, j], recv_sem=y_r.at[at, way, j],
            device_id={"rcv": row_dev((2, 1, 1, 2)[j] * sign)}, device_id_type=MESH)

    def to_sibling(blk, rows):
        pltpu.make_async_remote_copy(
            src_ref=pb.at[blk, rows, :], dst_ref=pb.at[blk, rows, :],
            send_sem=d_s.at[blk], recv_sem=d_r.at[blk],
            device_id={"rcv": sib}, device_id_type=MESH).start()

    def ring_recv(part_set, j):
        for way in range(2):
            sign = -1 if way else 1
            ring_copy(part_set, way, j).wait_recv()
            if j == 0:
                ring_copy(part_set, way, 2).start()
                ring_copy(part_set, way, 3).start()
            to_sibling(part_set[0], ring_rows(part_set, -(2, 1, 3, 4)[j] * sign, way, j))

    def ring_start(part_set):
        for j in range(2):
            for way in range(2):
                ring_copy(part_set, way, j).start()
        to_sibling(part_set[0], ring_rows(part_set, 0, 0, 0))

    def correlate(blk):
        wait_rows(pb.at[blk, pl.ds(0, FREQ), :], d_r.at[blk])
        for half_span in range(2):
            for n in range(2):
                cols = slice(half_span * SPAN + n * 256, half_span * SPAN + (n + 1) * 256)
                part[blk, half_span, :, n * 256:(n + 1) * 256] = lax.dot_general(
                    pb[blk], st[:, cols], (((0,), (0,)), ((), ())),
                    preferred_element_type=jnp.float32).astype(jnp.bfloat16)
            for d in (4, 5, 3, 6, 2, 1, 7):
                s2 = shot(d)
                pltpu.make_async_remote_copy(
                    src_ref=part.at[blk, half_span, pl.ds(pl.multiple_of(s2 * ROWS, ROWS), ROWS), :],
                    dst_ref=rb.at[blk, half_span, (d - 1) * ROWS:d * ROWS, :],
                    send_sem=rs_s.at[blk, half_span], recv_sem=rs_r.at[blk, half_span],
                    device_id={"shot": s2}, device_id_type=MESH).start()

    def stack(blk):
        mine = pl.ds(pl.multiple_of(s * ROWS, ROWS), ROWS)
        for l in range(LAGS):
            half_span, n = l // half, l % half
            if n == 0:
                wait_rows(rb.at[blk, half_span], rs_r.at[blk, half_span])
            cols = slice(n * CHAN, (n + 1) * CHAN)
            acc = part[blk, half_span, mine, cols].astype(jnp.float32)
            for d in range(SHOTS - 1):
                acc = acc + rb[blk, half_span, d * ROWS:(d + 1) * ROWS, cols].astype(jnp.float32)
            res[blk, :, l, :] = acc

    for blk, root in ((0, 0), (1, CHIPS - 1)):
        @pl.when(zh == root // N_Y)
        def _():
            @pl.when(y != root % N_Y)
            def _():
                wait_rows(pb.at[blk, my_rows, :], scat_r.at[blk])
            column_send(blk)

    mid_row(0)
    mid_row(1)

    sets = [(0, 0, GROUP, 0), (1, 0, GROUP, 1), (2, 0, HALF, 2), (2, HALF, HALF, 3)]
    for blk, root in ((0, 0), (1, CHIPS - 1)):
        @pl.when(zh != root // N_Y)
        def _():
            wait_rows(pb.at[blk, my_rows, :], z_r.at[blk])
        ring_start(sets[blk])
    for h in range(2):
        mid_column(h)
        ring_start(sets[2 + h])
    for part_set in sets:
        ring_recv(part_set, 0)
    for blk in range(BLOCKS):
        for part_set in sets:
            if part_set[0] == blk:
                for j in range(1, 4):
                    ring_recv(part_set, j)
        correlate(blk)
    for blk in range(BLOCKS):
        stack(blk)

    for b in range(BLOCKS):
        owner = jnp.full((ROWS, LAGS, CHAN), owners_ref[b], jnp.int32)
        out_ref[b] = jnp.where(owner == 0, res[0], jnp.where(owner == N_RCV - 1, res[1], res[2]))

    swap.wait_send()
    for h in range(2):
        wait_rows(mr.at[h], mid_s.at[h])
        for d in range(1, N_ZH):
            mid_copy(h, d).wait_send()
    for blk, root in ((0, 0), (1, CHIPS - 1)):
        @pl.when(q == root)
        def _():
            wait_rows(pb.at[blk, pl.ds(0, FREQ - GROUP), :], scat_s.at[blk])

        @pl.when(zh == root // N_Y)
        def _():
            wait_rows(pb.at[blk, pl.ds(0, (N_ZH - 1) * GROUP), :], z_s.at[blk])
    for part_set in sets:
        for j in range(4):
            for way in range(2):
                ring_copy(part_set, way, j).wait_send()
    for blk in range(BLOCKS):
        wait_rows(pb.at[blk, pl.ds(0, FREQ), :], d_s.at[blk])
        for half_span in range(2):
            wait_rows(rb.at[blk, half_span], rs_s.at[blk, half_span])


def on_device(records, live_mask, owners):
    bf16, f32 = jnp.bfloat16, jnp.float32
    dma = pltpu.SemaphoreType.DMA
    return pl.pallas_call(
        kernel,
        out_shape=jax.ShapeDtypeStruct((BLOCKS, ROWS, LAGS, CHAN), f32),
        in_specs=[
            pl.BlockSpec(memory_space=pltpu.SMEM),
            pl.BlockSpec(memory_space=pltpu.HBM),
            pl.BlockSpec(memory_space=pltpu.HBM),
            pl.BlockSpec(memory_space=pltpu.HBM),
        ],
        out_specs=pl.BlockSpec(memory_space=pltpu.VMEM),
        scratch_shapes=[
            pltpu.VMEM((1, CHAN), jnp.int32),
            pltpu.VMEM((FREQ, LAGS), f32),
            pltpu.VMEM((2, FREQ, CHAN), bf16),
            pltpu.VMEM((2, FREQ, CHAN), bf16),
            pltpu.VMEM((FREQ, CHAN), bf16),
            pltpu.VMEM((FREQ, CHAN), bf16),
            pltpu.VMEM((2, (N_Y - 1) * HALF, CHAN), bf16),
            pltpu.VMEM((2, HALF, CHAN), bf16),
            pltpu.VMEM((2, N_ZH - 1, HALF, CHAN), bf16),
            pltpu.VMEM((BLOCKS, 2 * FREQ, CHAN), bf16),
            pltpu.VMEM((2 * FREQ, WIDE), bf16),
            pltpu.VMEM((BLOCKS, 2, CHAN, SPAN), bf16),
            pltpu.VMEM((BLOCKS, 2, (SHOTS - 1) * ROWS, SPAN), bf16),
            pltpu.VMEM((BLOCKS, ROWS, LAGS, CHAN), f32),
            dma, dma, dma, dma, dma, dma((2,)), dma((2,)), dma((2,)), dma((2,)),
            dma((2, N_ZH - 1)), dma((2, N_ZH - 1)), dma((2,)), dma((2,)),
            dma((4, 2, 4)), dma((4, 2, 4)),
            dma((BLOCKS,)), dma((BLOCKS,)), dma((BLOCKS, 2)), dma((BLOCKS, 2)),
        ],
        cost_estimate=pl.CostEstimate(flops=1_700_000_000, bytes_accessed=1_500_000, transcendentals=0),
        compiler_params=pltpu.CompilerParams(
            collective_id=0, has_side_effects=True, vmem_limit_bytes=64 * 2**20),
    )(owners, live_mask, jnp.asarray(lag_tables()), records.reshape(2, FREQ, CHAN))


def solution(mesh):
    in_specs = (P(None, "shot", None, "rcv"), P("shot", "rcv"), P())
    out_specs = P(None, "shot", None, "rcv")
    return jax.shard_map(
        on_device, mesh=mesh, in_specs=in_specs, out_specs=out_specs, check_vma=False
    )
```

```python
import functools
import math

import jax
import jax.numpy as jnp
import numpy as np
from jax import lax
from jax.experimental import pallas as pl
from jax.experimental.pallas import tpu as pltpu
from jax.sharding import PartitionSpec as P

FREQ = 1024
CHAN = 128
BLOCKS = 3
LAGS = 8
STRIDE = 16
N_ZH = 4
N_Y = 8
CHIPS = N_ZH * N_Y
N_RCV = 2 * CHIPS
SHOTS = 8
GROUP = FREQ // N_Y
HALF = GROUP // 2
ROWS = CHAN // SHOTS
WIDE = LAGS * CHAN
SPAN = WIDE // 2
MESH = pl.DeviceIdType.MESH


def lag_tables():
    f32 = np.float32
    freq_index = np.arange(FREQ, dtype=f32)
    lag_index = np.arange(LAGS, dtype=f32)
    shifts = (lag_index - f32(LAGS // 2)) * f32(STRIDE) + f32(STRIDE // 2)
    taper = f32(0.54) + f32(0.46) * np.cos(f32(2.0 * math.pi) * (lag_index + f32(0.5)) / f32(LAGS) - f32(math.pi))
    phases = f32(math.pi) * freq_index[:, None] * shifts[None, :] / f32(FREQ)
    weights = taper[None, :] / np.sqrt(f32(SHOTS * FREQ))
    half = LAGS // 2
    cos_table = (np.cos(phases) * weights)[:, :half]
    sin_table = (np.sin(phases) * weights)[:, :half]
    return np.concatenate([cos_table, sin_table], axis=1).astype(f32)


def kernel(
    owners_ref, mask_hbm, tab_hbm, rec_hbm, out_ref,
    mask_ref, tab_ref, rec, own, xb, ms, mr, mp, mz, pb, st, part, rb, zb, pq, xs, res,
    mask_sem, tab_sem, load_sem, sib_s, sib_r, scat_s, scat_r, mid_s, mid_r,
    mz_s, mz_r, z_s, z_r, y_s, y_r, d_s, d_r, rs_s, rs_r, p_s, p_r, x_s, x_r,
):
    r = lax.axis_index("rcv")
    s = lax.axis_index("shot")
    q = lax.div(r, 2)
    core = lax.rem(r, 2)
    zh = lax.div(q, N_Y)
    y = lax.rem(q, N_Y)
    sib = r + 1 - 2 * core

    def row_dev(d):
        return (zh * N_Y + lax.rem(y + d + N_Y, N_Y)) * 2 + core

    def column_dev(d):
        return (lax.rem(zh + d, N_ZH) * N_Y + y) * 2 + core

    def shot(d):
        return lax.rem(s + d, SHOTS)

    barrier = pltpu.get_barrier_semaphore()

    def greet(dev):
        pl.semaphore_signal(barrier, inc=1, device_id=dev, device_id_type=MESH)

    load = pltpu.make_async_copy(rec_hbm, rec, load_sem)
    load.start()
    load_mask = pltpu.make_async_copy(mask_hbm, mask_ref, mask_sem)
    load_mask.start()
    load_tab = pltpu.make_async_copy(tab_hbm, tab_ref, tab_sem)
    load_tab.start()
    for d in range(N_Y - 1, 0, -1):
        greet({"rcv": row_dev(d)})
    for d in range(1, N_ZH):
        greet({"rcv": column_dev(d)})
    greet({"rcv": sib})
    for d in range(1, SHOTS):
        greet({"shot": shot(d)})

    load.wait()

    def add_power(i, acc):
        rows = pl.ds(pl.multiple_of(i * 64, 64), 64)
        for p in range(2):
            v = rec[p, rows, :].astype(jnp.float32)
            v = v * v
            for j in range(8):
                acc = acc + v[8 * j:8 * j + 8]
        return acc

    total = lax.fori_loop(0, FREQ // 64, add_power, jnp.zeros((8, CHAN), jnp.float32))
    power = jnp.sum(total, axis=0, keepdims=True) * (1.0 / (2 * FREQ))
    load_mask.wait()
    gain = mask_ref[...].astype(jnp.float32) / jnp.sqrt(power + 1e-06)

    def whiten_part(p):
        def body(i, carry):
            rows = pl.ds(pl.multiple_of(i * 128, 128), 128)
            own[p, rows, :] = (rec[p, rows, :].astype(jnp.float32) * gain).astype(jnp.bfloat16)
            return carry
        lax.fori_loop(0, FREQ // 128, body, 0)

    whiten_part(1 - core)
    pl.semaphore_wait(barrier, N_Y - 1 + N_ZH - 1 + 1 + SHOTS - 1)
    swap = pltpu.make_async_remote_copy(
        src_ref=own.at[1 - core], dst_ref=xb, send_sem=sib_s, recv_sem=sib_r,
        device_id={"rcv": sib}, device_id_type=MESH)
    swap.start()
    whiten_part(core)
    swap.wait_recv()

    base = core * FREQ

    def rows_of(start, size):
        return pl.ds(pl.multiple_of(start, 16), size)

    my_rows = rows_of(base + y * GROUP, GROUP)

    def scatter(blk, src):
        for d in range(1, N_Y):
            row = lax.rem(y + d, N_Y) * GROUP
            pltpu.make_async_remote_copy(
                src_ref=src.at[rows_of(row, GROUP), :],
                dst_ref=pb.at[blk, rows_of(base + row, GROUP), :],
                send_sem=scat_s.at[blk], recv_sem=scat_r.at[blk],
                device_id={"rcv": row_dev(d)}, device_id_type=MESH).start()
        pb[blk, my_rows, :] = src[rows_of(y * GROUP, GROUP), :]

    @pl.when(r == 0)
    def _():
        scatter(0, own.at[0])

    @pl.when(r == 1)
    def _():
        scatter(0, xb)

    @pl.when(r == N_RCV - 1)
    def _():
        scatter(1, own.at[1])

    @pl.when(r == N_RCV - 2)
    def _():
        scatter(1, xb)

    mid = owners_ref[0] + owners_ref[1] + owners_ref[2] - (N_RCV - 1)
    is_me = jnp.where(mid == r, 1.0, 0.0).astype(jnp.float32)
    is_sib = jnp.where(mid == sib, 1.0, 0.0).astype(jnp.float32)

    def pick(i, carry):
        rows = pl.ds(pl.multiple_of(i * 128, 128), 128)
        mine = own[core, rows, :].astype(jnp.float32) * is_me
        other = xb[rows, :].astype(jnp.float32) * is_sib
        ms[rows, :] = (mine + other).astype(jnp.bfloat16)
        return carry

    lax.fori_loop(0, FREQ // 128, pick, 0)

    for h in range(2):
        for d in (4, 3, 5, 2, 6, 1, 7):
            pltpu.make_async_remote_copy(
                src_ref=ms.at[rows_of(lax.rem(y + d, N_Y) * GROUP + h * HALF, HALF), :],
                dst_ref=mr.at[h, (d - 1) * HALF:d * HALF, :],
                send_sem=mid_s.at[h], recv_sem=mid_r.at[h],
                device_id={"rcv": row_dev(d)}, device_id_type=MESH).start()

    half = LAGS // 2

    def steer(i, carry):
        rows = pl.ds(pl.multiple_of(i * 16, 16), 16)
        low = pl.ds(pl.multiple_of(FREQ + i * 16, 16), 16)
        a = rec[0, rows, :].astype(jnp.float32) * gain
        b = rec[1, rows, :].astype(jnp.float32) * gain
        for l in range(half):
            c = jnp.broadcast_to(tab_ref[rows, l:l + 1], (16, CHAN))
            t = jnp.broadcast_to(tab_ref[rows, half + l:half + l + 1], (16, CHAN))
            ac, bt, at, bc = a * c, b * t, a * t, b * c
            near = slice(l * CHAN, (l + 1) * CHAN)
            far = slice((LAGS - 1 - l) * CHAN, (LAGS - l) * CHAN)
            st[rows, near] = (ac - bt).astype(jnp.bfloat16)
            st[rows, far] = (ac + bt).astype(jnp.bfloat16)
            st[low, near] = (at + bc).astype(jnp.bfloat16)
            st[low, far] = (bc - at).astype(jnp.bfloat16)
        return carry

    load_tab.wait()
    lax.fori_loop(0, FREQ // 16, steer, 0)

    def wait_rows(ref, sem):
        pltpu.make_async_copy(ref, ref, sem).wait()

    def column_send(blk):
        for d in range(1, N_ZH):
            pltpu.make_async_remote_copy(
                src_ref=pb.at[blk, my_rows, :], dst_ref=pb.at[blk, my_rows, :],
                send_sem=z_s.at[blk], recv_sem=z_r.at[blk],
                device_id={"rcv": column_dev(d)}, device_id_type=MESH).start()

    def mid_copy(h, d):
        return pltpu.make_async_remote_copy(
            src_ref=mp.at[h], dst_ref=mz.at[h, d - 1],
            send_sem=mz_s.at[h, d - 1], recv_sem=mz_r.at[h, d - 1],
            device_id={"rcv": column_dev(d)}, device_id_type=MESH)

    def mid_row(h):
        wait_rows(mr.at[h], mid_r.at[h])
        acc = ms[rows_of(y * GROUP + h * HALF, HALF), :]
        for d in range(N_Y - 1):
            acc = acc + mr[h, d * HALF:(d + 1) * HALF, :]
        mp[h] = acc
        for d in (2, 1, 3):
            mid_copy(h, d).start()

    def mid_column(h):
        acc = mp[h]
        for d in range(1, N_ZH):
            mid_copy(h, d).wait_recv()
            acc = acc + mz[h, d - 1]
        pb[2, rows_of(base + y * GROUP + h * HALF, HALF), :] = acc

    def ring_at(offset):
        return lax.rem(y + N_Y + offset, N_Y)

    def ring_rows(part_set, offset, way, j):
        _, low, size, _ = part_set
        start = base + ring_at(offset) * GROUP + low
        if j < 3:
            return rows_of(start, size)
        return rows_of(start + way * (size // 2), size // 2)

    def ring_copy(part_set, way, j):
        blk, _, _, at = part_set
        sign = -1 if way else 1
        rows = ring_rows(part_set, 0 if j < 2 else -2 * sign, way, j)
        return pltpu.make_async_remote_copy(
            src_ref=pb.at[blk, rows, :], dst_ref=pb.at[blk, rows, :],
            send_sem=y_s.at[at, way, j], recv_sem=y_r.at[at, way, j],
            device_id={"rcv": row_dev((2, 1, 1, 2)[j] * sign)}, device_id_type=MESH)

    def to_sibling(blk, rows):
        pltpu.make_async_remote_copy(
            src_ref=pb.at[blk, rows, :], dst_ref=pb.at[blk, rows, :],
            send_sem=d_s.at[blk], recv_sem=d_r.at[blk],
            device_id={"rcv": sib}, device_id_type=MESH).start()

    def ring_recv(part_set, j):
        for way in range(2):
            sign = -1 if way else 1
            ring_copy(part_set, way, j).wait_recv()
            if j == 0:
                ring_copy(part_set, way, 2).start()
                ring_copy(part_set, way, 3).start()
            to_sibling(part_set[0], ring_rows(part_set, -(2, 1, 3, 4)[j] * sign, way, j))

    def ring_start(part_set):
        for j in range(2):
            for way in range(2):
                ring_copy(part_set, way, j).start()
        to_sibling(part_set[0], ring_rows(part_set, 0, 0, 0))

    def part_row(s2):
        return rows_of(lax.rem(s2, 2) * (CHAN // 2) + lax.div(s2, 2) * ROWS, ROWS)

    mine = part_row(s)
    odd = lax.rem(s, 2)
    pair = s + 1 - 2 * odd
    my_side = rows_of(odd * (CHAN // 2), CHAN // 2)
    pair_side = rows_of((1 - odd) * (CHAN // 2), CHAN // 2)
    spans = range(2)

    def direct_copy(hs, d):
        s2 = shot(d)
        return pltpu.make_async_remote_copy(
            src_ref=part.at[2, hs, part_row(s2), :],
            dst_ref=rb.at[hs, (d - 1) * ROWS:d * ROWS, :],
            send_sem=rs_s.at[hs], recv_sem=rs_r.at[hs],
            device_id={"shot": s2}, device_id_type=MESH)

    def pair_copy(blk, hs):
        return pltpu.make_async_remote_copy(
            src_ref=part.at[blk, hs, pair_side, :], dst_ref=zb.at[blk, hs],
            send_sem=p_s.at[blk, hs], recv_sem=p_r.at[blk, hs],
            device_id={"shot": pair}, device_id_type=MESH)

    def line_copy(blk, hs, d):
        x2 = lax.rem(lax.div(s, 2) + d, SHOTS // 2)
        return pltpu.make_async_remote_copy(
            src_ref=pq.at[blk, hs, rows_of(x2 * ROWS, ROWS), :], dst_ref=xs.at[blk, hs, d - 1],
            send_sem=x_s.at[blk, hs, d - 1], recv_sem=x_r.at[blk, hs, d - 1],
            device_id={"shot": x2 * 2 + odd}, device_id_type=MESH)

    def correlate(blk):
        wait_rows(pb.at[blk, pl.ds(0, FREQ), :], d_r.at[blk])
        for hs in spans:
            for n in range(2):
                cols = slice(hs * SPAN + n * 256, hs * SPAN + (n + 1) * 256)
                sums = lax.dot_general(
                    pb[blk], st[:, cols], (((0,), (0,)), ((), ())),
                    preferred_element_type=jnp.float32).astype(jnp.bfloat16)
                for s2 in range(SHOTS):
                    row = s2 % 2 * (CHAN // 2) + s2 // 2 * ROWS
                    part[blk, hs, row:row + ROWS, n * 256:(n + 1) * 256] = sums[s2 * ROWS:(s2 + 1) * ROWS]
            if blk < 2:
                pair_copy(blk, hs).start()
            else:
                for d in (4, 5, 3, 6, 2, 1, 7):
                    direct_copy(hs, d).start()

    def pair_sum(blk):
        for hs in spans:
            pair_copy(blk, hs).wait_recv()
            both = part[blk, hs, my_side, :].astype(jnp.float32) + zb[blk, hs].astype(jnp.float32)
            pq[blk, hs] = both.astype(jnp.bfloat16)
            for d in (2, 1, 3):
                line_copy(blk, hs, d).start()

    def put(blk, hs, acc):
        for n in range(half):
            res[blk, :, hs * half + n, :] = acc[:, n * CHAN:(n + 1) * CHAN]

    def stack(blk):
        for hs in spans:
            acc = part[blk, hs, mine, :].astype(jnp.float32)
            if blk < 2:
                acc = acc + zb[blk, hs, rows_of(lax.div(s, 2) * ROWS, ROWS), :].astype(jnp.float32)
                for d in range(1, SHOTS // 2):
                    line_copy(blk, hs, d).wait_recv()
                    acc = acc + xs[blk, hs, d - 1].astype(jnp.float32)
            else:
                wait_rows(rb.at[hs], rs_r.at[hs])
                for d in range(SHOTS - 1):
                    acc = acc + rb[hs, d * ROWS:(d + 1) * ROWS, :].astype(jnp.float32)
            put(blk, hs, acc)

    for blk, root in ((0, 0), (1, CHIPS - 1)):
        @pl.when(zh == root // N_Y)
        def _():
            @pl.when(y != root % N_Y)
            def _():
                wait_rows(pb.at[blk, my_rows, :], scat_r.at[blk])
            column_send(blk)

    mid_row(0)
    mid_row(1)

    sets = [(0, 0, GROUP, 0), (1, 0, GROUP, 1), (2, 0, HALF, 2), (2, HALF, HALF, 3)]
    for blk, root in ((0, 0), (1, CHIPS - 1)):
        @pl.when(zh != root // N_Y)
        def _():
            wait_rows(pb.at[blk, my_rows, :], z_r.at[blk])
        ring_start(sets[blk])
    for h in range(2):
        mid_column(h)
        ring_start(sets[2 + h])
    def ring_rest(part_set):
        for j in range(1, 4):
            ring_recv(part_set, j)

    for part_set in sets[:3]:
        ring_recv(part_set, 0)
    ring_rest(sets[0])
    ring_recv(sets[3], 0)
    correlate(0)
    ring_rest(sets[1])
    correlate(1)
    pair_sum(0)
    ring_rest(sets[2])
    pair_sum(1)
    ring_rest(sets[3])
    correlate(2)
    for blk in range(BLOCKS):
        stack(blk)

    for b in range(BLOCKS):
        owner = jnp.full((ROWS, LAGS, CHAN), owners_ref[b], jnp.int32)
        out_ref[b] = jnp.where(owner == 0, res[0], jnp.where(owner == N_RCV - 1, res[1], res[2]))

    swap.wait_send()
    for h in range(2):
        wait_rows(mr.at[h], mid_s.at[h])
        for d in range(1, N_ZH):
            mid_copy(h, d).wait_send()
    for blk, root in ((0, 0), (1, CHIPS - 1)):
        @pl.when(q == root)
        def _():
            wait_rows(pb.at[blk, pl.ds(0, FREQ - GROUP), :], scat_s.at[blk])

        @pl.when(zh == root // N_Y)
        def _():
            wait_rows(pb.at[blk, pl.ds(0, (N_ZH - 1) * GROUP), :], z_s.at[blk])
    for part_set in sets:
        for j in range(4):
            for way in range(2):
                ring_copy(part_set, way, j).wait_send()
    for blk in range(BLOCKS):
        wait_rows(pb.at[blk, pl.ds(0, FREQ), :], d_s.at[blk])
    for hs in spans:
        wait_rows(rb.at[hs], rs_s.at[hs])
        for blk in range(2):
            pair_copy(blk, hs).wait_send()
            for d in range(1, SHOTS // 2):
                line_copy(blk, hs, d).wait_send()


def on_device(records, live_mask, owners):
    bf16, f32 = jnp.bfloat16, jnp.float32
    dma = pltpu.SemaphoreType.DMA
    return pl.pallas_call(
        kernel,
        out_shape=pltpu.VMEM((BLOCKS, ROWS, LAGS, CHAN), f32),
        in_specs=[
            pl.BlockSpec(memory_space=pltpu.SMEM),
            pl.BlockSpec(memory_space=pltpu.HBM),
            pl.BlockSpec(memory_space=pltpu.HBM),
            pl.BlockSpec(memory_space=pltpu.HBM),
        ],
        out_specs=pl.BlockSpec(memory_space=pltpu.VMEM),
        scratch_shapes=[
            pltpu.VMEM((1, CHAN), jnp.int32),
            pltpu.VMEM((FREQ, LAGS), f32),
            pltpu.VMEM((2, FREQ, CHAN), bf16),
            pltpu.VMEM((2, FREQ, CHAN), bf16),
            pltpu.VMEM((FREQ, CHAN), bf16),
            pltpu.VMEM((FREQ, CHAN), bf16),
            pltpu.VMEM((2, (N_Y - 1) * HALF, CHAN), bf16),
            pltpu.VMEM((2, HALF, CHAN), bf16),
            pltpu.VMEM((2, N_ZH - 1, HALF, CHAN), bf16),
            pltpu.VMEM((BLOCKS, 2 * FREQ, CHAN), bf16),
            pltpu.VMEM((2 * FREQ, WIDE), bf16),
            pltpu.VMEM((BLOCKS, 2, CHAN, SPAN), bf16),
            pltpu.VMEM((2, (SHOTS - 1) * ROWS, SPAN), bf16),
            pltpu.VMEM((2, 2, CHAN // 2, SPAN), bf16),
            pltpu.VMEM((2, 2, CHAN // 2, SPAN), bf16),
            pltpu.VMEM((2, 2, SHOTS // 2 - 1, ROWS, SPAN), bf16),
            pltpu.VMEM((BLOCKS, ROWS, LAGS, CHAN), f32),
            dma, dma, dma, dma, dma, dma((2,)), dma((2,)), dma((2,)), dma((2,)),
            dma((2, N_ZH - 1)), dma((2, N_ZH - 1)), dma((2,)), dma((2,)),
            dma((4, 2, 4)), dma((4, 2, 4)),
            dma((BLOCKS,)), dma((BLOCKS,)), dma((2,)), dma((2,)), dma((2, 2)), dma((2, 2)),
            dma((2, 2, SHOTS // 2 - 1)), dma((2, 2, SHOTS // 2 - 1)),
        ],
        cost_estimate=pl.CostEstimate(flops=1_700_000_000, bytes_accessed=1_500_000, transcendentals=0),
        compiler_params=pltpu.CompilerParams(
            collective_id=0, has_side_effects=True, vmem_limit_bytes=62 * 2**20),
    )(owners, live_mask, jnp.asarray(lag_tables()), records.reshape(2, FREQ, CHAN))


def solution(mesh):
    in_specs = (P(None, "shot", None, "rcv"), P("shot", "rcv"), P())
    out_specs = P(None, "shot", None, "rcv")
    return jax.shard_map(
        on_device, mesh=mesh, in_specs=in_specs, out_specs=out_specs, check_vma=False
    )
```

```python
import functools
import math

import jax
import jax.numpy as jnp
import numpy as np
from jax import lax
from jax.experimental import pallas as pl
from jax.experimental.pallas import tpu as pltpu
from jax.sharding import PartitionSpec as P

FREQ = 1024
CHAN = 128
BLOCKS = 3
LAGS = 8
STRIDE = 16
N_ZH = 4
N_Y = 8
CHIPS = N_ZH * N_Y
N_RCV = 2 * CHIPS
SHOTS = 8
GROUP = FREQ // N_Y
HALF = GROUP // 2
ROWS = CHAN // SHOTS
WIDE = LAGS * CHAN
SPAN = WIDE // 2
MESH = pl.DeviceIdType.MESH


def lag_tables():
    f32 = np.float32
    freq_index = np.arange(FREQ, dtype=f32)
    lag_index = np.arange(LAGS, dtype=f32)
    shifts = (lag_index - f32(LAGS // 2)) * f32(STRIDE) + f32(STRIDE // 2)
    taper = f32(0.54) + f32(0.46) * np.cos(f32(2.0 * math.pi) * (lag_index + f32(0.5)) / f32(LAGS) - f32(math.pi))
    phases = f32(math.pi) * freq_index[:, None] * shifts[None, :] / f32(FREQ)
    weights = taper[None, :] / np.sqrt(f32(SHOTS * FREQ))
    half = LAGS // 2
    cos_table = (np.cos(phases) * weights)[:, :half]
    sin_table = (np.sin(phases) * weights)[:, :half]
    return np.concatenate([cos_table, sin_table], axis=1).astype(f32)


def kernel(
    owners_ref, mask_hbm, tab_hbm, rec_hbm, out_ref,
    mask_ref, tab_ref, rec, own, xb, ms, mr, mp, mz, pb, st, part, rb, res,
    mask_sem, tab_sem, load_sem, sib_s, sib_r, scat_s, scat_r, mid_s, mid_r,
    ready, mz_s, mz_r, z_s, z_r, y_s, y_r, d_s, d_r, rs_s, rs_r,
):
    r = lax.axis_index("rcv")
    s = lax.axis_index("shot")
    q = lax.div(r, 2)
    core = lax.rem(r, 2)
    zh = lax.div(q, N_Y)
    y = lax.rem(q, N_Y)
    sib = r + 1 - 2 * core

    def row_dev(d):
        return (zh * N_Y + lax.rem(y + d + N_Y, N_Y)) * 2 + core

    def column_dev(d):
        return (lax.rem(zh + d, N_ZH) * N_Y + y) * 2 + core

    def row_z(z2):
        return (z2 * N_Y + y) * 2 + core

    def shot(d):
        return lax.rem(s + d, SHOTS)

    barrier = pltpu.get_barrier_semaphore()

    def greet(dev):
        pl.semaphore_signal(barrier, inc=1, device_id=dev, device_id_type=MESH)

    load = pltpu.make_async_copy(rec_hbm, rec, load_sem)
    load.start()
    load_mask = pltpu.make_async_copy(mask_hbm, mask_ref, mask_sem)
    load_mask.start()
    load_tab = pltpu.make_async_copy(tab_hbm, tab_ref, tab_sem)
    load_tab.start()
    for d in range(N_Y - 1, 0, -1):
        greet({"rcv": row_dev(d)})
    for z2 in range(1, N_ZH):
        @pl.when(zh < z2)
        def _():
            greet({"rcv": row_z(z2)})
    greet({"rcv": sib})
    for d in range(1, SHOTS):
        greet({"shot": shot(d)})

    load.wait()

    def add_power(i, acc):
        rows = pl.ds(pl.multiple_of(i * 64, 64), 64)
        for p in range(2):
            v = rec[p, rows, :].astype(jnp.float32)
            v = v * v
            for j in range(8):
                acc = acc + v[8 * j:8 * j + 8]
        return acc

    total = lax.fori_loop(0, FREQ // 64, add_power, jnp.zeros((8, CHAN), jnp.float32))
    power = jnp.sum(total, axis=0, keepdims=True) * (1.0 / (2 * FREQ))
    load_mask.wait()
    gain = mask_ref[...].astype(jnp.float32) / jnp.sqrt(power + 1e-06)

    def whiten_part(p):
        def body(i, carry):
            rows = pl.ds(pl.multiple_of(i * 128, 128), 128)
            own[p, rows, :] = (rec[p, rows, :].astype(jnp.float32) * gain).astype(jnp.bfloat16)
            return carry
        lax.fori_loop(0, FREQ // 128, body, 0)

    whiten_part(1 - core)
    pl.semaphore_wait(barrier, N_Y - 1 + zh + 1 + SHOTS - 1)
    swap = pltpu.make_async_remote_copy(
        src_ref=own.at[1 - core], dst_ref=xb, send_sem=sib_s, recv_sem=sib_r,
        device_id={"rcv": sib}, device_id_type=MESH)
    swap.start()
    for z2 in range(N_ZH - 1):
        @pl.when(zh > z2)
        def _():
            pl.semaphore_signal(ready.at[zh], inc=1, device_id={"rcv": row_z(z2)}, device_id_type=MESH)

    whiten_part(core)
    swap.wait_recv()

    base = core * FREQ

    def rows_of(start, size):
        return pl.ds(pl.multiple_of(start, 16), size)

    my_rows = rows_of(base + y * GROUP, GROUP)

    def scatter(blk, src):
        for d in range(1, N_Y):
            row = lax.rem(y + d, N_Y) * GROUP
            pltpu.make_async_remote_copy(
                src_ref=src.at[rows_of(row, GROUP), :],
                dst_ref=pb.at[blk, rows_of(base + row, GROUP), :],
                send_sem=scat_s.at[blk], recv_sem=scat_r.at[blk],
                device_id={"rcv": row_dev(d)}, device_id_type=MESH).start()
        pb[blk, my_rows, :] = src[rows_of(y * GROUP, GROUP), :]

    @pl.when(r == 0)
    def _():
        scatter(0, own.at[0])

    @pl.when(r == 1)
    def _():
        scatter(0, xb)

    @pl.when(r == N_RCV - 1)
    def _():
        scatter(1, own.at[1])

    @pl.when(r == N_RCV - 2)
    def _():
        scatter(1, xb)

    mid = owners_ref[0] + owners_ref[1] + owners_ref[2] - (N_RCV - 1)
    is_me = jnp.where(mid == r, 1.0, 0.0).astype(jnp.float32)
    is_sib = jnp.where(mid == sib, 1.0, 0.0).astype(jnp.float32)

    def pick(i, carry):
        rows = pl.ds(pl.multiple_of(i * 128, 128), 128)
        mine = own[core, rows, :].astype(jnp.float32) * is_me
        other = xb[rows, :].astype(jnp.float32) * is_sib
        ms[rows, :] = (mine + other).astype(jnp.bfloat16)
        return carry

    lax.fori_loop(0, FREQ // 128, pick, 0)

    for h in range(2):
        for d in (4, 3, 5, 2, 6, 1, 7):
            pltpu.make_async_remote_copy(
                src_ref=ms.at[rows_of(lax.rem(y + d, N_Y) * GROUP + h * HALF, HALF), :],
                dst_ref=mr.at[h, (d - 1) * HALF:d * HALF, :],
                send_sem=mid_s.at[h], recv_sem=mid_r.at[h],
                device_id={"rcv": row_dev(d)}, device_id_type=MESH).start()

    half = LAGS // 2

    def steer(i, carry):
        rows = pl.ds(pl.multiple_of(i * 16, 16), 16)
        low = pl.ds(pl.multiple_of(FREQ + i * 16, 16), 16)
        a = rec[0, rows, :].astype(jnp.float32) * gain
        b = rec[1, rows, :].astype(jnp.float32) * gain
        for l in range(half):
            c = jnp.broadcast_to(tab_ref[rows, l:l + 1], (16, CHAN))
            t = jnp.broadcast_to(tab_ref[rows, half + l:half + l + 1], (16, CHAN))
            ac, bt, at, bc = a * c, b * t, a * t, b * c
            near = slice(l * CHAN, (l + 1) * CHAN)
            far = slice((LAGS - 1 - l) * CHAN, (LAGS - l) * CHAN)
            st[rows, near] = (ac - bt).astype(jnp.bfloat16)
            st[rows, far] = (ac + bt).astype(jnp.bfloat16)
            st[low, near] = (at + bc).astype(jnp.bfloat16)
            st[low, far] = (bc - at).astype(jnp.bfloat16)
        return carry

    load_tab.wait()
    lax.fori_loop(0, FREQ // 16, steer, 0)

    def wait_rows(ref, sem):
        pltpu.make_async_copy(ref, ref, sem).wait()

    def column_send(blk, z2):
        pltpu.make_async_remote_copy(
            src_ref=pb.at[blk, my_rows, :], dst_ref=pb.at[blk, my_rows, :],
            send_sem=z_s.at[blk], recv_sem=z_r.at[blk],
            device_id={"rcv": row_z(z2)}, device_id_type=MESH).start()

    def mid_copy(h, d):
        return pltpu.make_async_remote_copy(
            src_ref=mp.at[h], dst_ref=mz.at[h, d - 1],
            send_sem=mz_s.at[h, d - 1], recv_sem=mz_r.at[h, d - 1],
            device_id={"rcv": column_dev(d)}, device_id_type=MESH)

    def mid_send(h, z2):
        @pl.when(zh != z2)
        def _():
            mid_copy(h, lax.rem(z2 - zh + N_ZH, N_ZH)).start()

    def mid_row(h):
        wait_rows(mr.at[h], mid_r.at[h])
        acc = ms[rows_of(y * GROUP + h * HALF, HALF), :]
        for d in range(N_Y - 1):
            acc = acc + mr[h, d * HALF:(d + 1) * HALF, :]
        mp[h] = acc
        mid_send(h, 0)
        mid_send(h, 1)

    def mid_column(h):
        acc = mp[h]
        for d in range(1, N_ZH):
            mid_copy(h, d).wait_recv()
            acc = acc + mz[h, d - 1]
        pb[2, rows_of(base + y * GROUP + h * HALF, HALF), :] = acc

    def ring_at(offset):
        return lax.rem(y + N_Y + offset, N_Y)

    def ring_rows(part_set, offset, way, j):
        _, low, size, _ = part_set
        start = base + ring_at(offset) * GROUP + low
        if j < 3:
            return rows_of(start, size)
        return rows_of(start + way * (size // 2), size // 2)

    def ring_copy(part_set, way, j):
        blk, _, _, at = part_set
        sign = -1 if way else 1
        rows = ring_rows(part_set, 0 if j < 2 else -2 * sign, way, j)
        return pltpu.make_async_remote_copy(
            src_ref=pb.at[blk, rows, :], dst_ref=pb.at[blk, rows, :],
            send_sem=y_s.at[at, way, j], recv_sem=y_r.at[at, way, j],
            device_id={"rcv": row_dev((2, 1, 1, 2)[j] * sign)}, device_id_type=MESH)

    def to_sibling(blk, rows):
        pltpu.make_async_remote_copy(
            src_ref=pb.at[blk, rows, :], dst_ref=pb.at[blk, rows, :],
            send_sem=d_s.at[blk], recv_sem=d_r.at[blk],
            device_id={"rcv": sib}, device_id_type=MESH).start()

    def ring_recv(part_set, j):
        for way in range(2):
            sign = -1 if way else 1
            ring_copy(part_set, way, j).wait_recv()
            if j == 0:
                ring_copy(part_set, way, 2).start()
                ring_copy(part_set, way, 3).start()
            to_sibling(part_set[0], ring_rows(part_set, -(2, 1, 3, 4)[j] * sign, way, j))

    def ring_start(part_set):
        for j in range(2):
            for way in range(2):
                ring_copy(part_set, way, j).start()
        to_sibling(part_set[0], ring_rows(part_set, 0, 0, 0))

    def correlate(blk):
        wait_rows(pb.at[blk, pl.ds(0, FREQ), :], d_r.at[blk])
        for half_span in range(2):
            for n in range(2):
                cols = slice(half_span * SPAN + n * 256, half_span * SPAN + (n + 1) * 256)
                part[blk, half_span, :, n * 256:(n + 1) * 256] = lax.dot_general(
                    pb[blk], st[:, cols], (((0,), (0,)), ((), ())),
                    preferred_element_type=jnp.float32).astype(jnp.bfloat16)
            for d in (4, 5, 3, 6, 2, 1, 7):
                s2 = shot(d)
                pltpu.make_async_remote_copy(
                    src_ref=part.at[blk, half_span, pl.ds(pl.multiple_of(s2 * ROWS, ROWS), ROWS), :],
                    dst_ref=rb.at[blk, half_span, (d - 1) * ROWS:d * ROWS, :],
                    send_sem=rs_s.at[blk, half_span], recv_sem=rs_r.at[blk, half_span],
                    device_id={"shot": s2}, device_id_type=MESH).start()

    def stack(blk):
        mine = pl.ds(pl.multiple_of(s * ROWS, ROWS), ROWS)
        for l in range(LAGS):
            half_span, n = l // half, l % half
            if n == 0:
                wait_rows(rb.at[blk, half_span], rs_r.at[blk, half_span])
            cols = slice(n * CHAN, (n + 1) * CHAN)
            acc = part[blk, half_span, mine, cols].astype(jnp.float32)
            for d in range(SHOTS - 1):
                acc = acc + rb[blk, half_span, d * ROWS:(d + 1) * ROWS, cols].astype(jnp.float32)
            res[blk, :, l, :] = acc

    sets = [(0, 0, GROUP, 0), (1, 0, GROUP, 1), (2, 0, HALF, 2), (2, HALF, HALF, 3)]

    def ring_rest(part_set):
        for j in range(1, 4):
            ring_recv(part_set, j)

    @pl.when(zh == 0)
    def _():
        @pl.when(y != 0)
        def _():
            wait_rows(pb.at[0, my_rows, :], scat_r.at[0])
        ring_start(sets[0])
        pl.semaphore_wait(ready.at[1], 1)
        column_send(0, 1)

    @pl.when(zh == 1)
    def _():
        wait_rows(pb.at[0, my_rows, :], z_r.at[0])
        ring_start(sets[0])

    @pl.when(zh < 2)
    def _():
        ring_recv(sets[0], 0)
        ring_rest(sets[0])
        correlate(0)

    @pl.when(zh == N_ZH - 1)
    def _():
        @pl.when(y != N_Y - 1)
        def _():
            wait_rows(pb.at[1, my_rows, :], scat_r.at[1])
        column_send(1, 0)
        column_send(1, 1)

    mid_row(0)
    mid_row(1)

    @pl.when(zh < 2)
    def _():
        pl.semaphore_wait(ready.at[2], 1)

    @pl.when(zh < 3)
    def _():
        pl.semaphore_wait(ready.at[3], 1)

    @pl.when(zh == 0)
    def _():
        column_send(0, 2)
        column_send(0, 3)

    @pl.when(zh == N_ZH - 1)
    def _():
        column_send(1, 2)

    for h in range(2):
        mid_send(h, 2)
        mid_send(h, 3)

    @pl.when(zh != N_ZH - 1)
    def _():
        wait_rows(pb.at[1, my_rows, :], z_r.at[1])
    ring_start(sets[1])

    @pl.when(zh >= 2)
    def _():
        wait_rows(pb.at[0, my_rows, :], z_r.at[0])
        ring_start(sets[0])

    for h in range(2):
        mid_column(h)
        ring_start(sets[2 + h])
    ring_recv(sets[1], 0)

    @pl.when(zh >= 2)
    def _():
        ring_recv(sets[0], 0)

    ring_recv(sets[2], 0)
    ring_recv(sets[3], 0)
    ring_rest(sets[1])
    correlate(1)

    @pl.when(zh >= 2)
    def _():
        ring_rest(sets[0])
        correlate(0)

    ring_rest(sets[2])
    ring_rest(sets[3])
    correlate(2)
    for blk in range(BLOCKS):
        stack(blk)

    for b in range(BLOCKS):
        owner = jnp.full((ROWS, LAGS, CHAN), owners_ref[b], jnp.int32)
        out_ref[b] = jnp.where(owner == 0, res[0], jnp.where(owner == N_RCV - 1, res[1], res[2]))

    swap.wait_send()
    for h in range(2):
        wait_rows(mr.at[h], mid_s.at[h])
        for d in range(1, N_ZH):
            mid_copy(h, d).wait_send()
    for blk, root in ((0, 0), (1, CHIPS - 1)):
        @pl.when(q == root)
        def _():
            wait_rows(pb.at[blk, pl.ds(0, FREQ - GROUP), :], scat_s.at[blk])

        @pl.when(zh == root // N_Y)
        def _():
            wait_rows(pb.at[blk, pl.ds(0, (N_ZH - 1) * GROUP), :], z_s.at[blk])
    for part_set in sets:
        for j in range(4):
            for way in range(2):
                ring_copy(part_set, way, j).wait_send()
    for blk in range(BLOCKS):
        wait_rows(pb.at[blk, pl.ds(0, FREQ), :], d_s.at[blk])
        for half_span in range(2):
            wait_rows(rb.at[blk, half_span], rs_s.at[blk, half_span])


def on_device(records, live_mask, owners):
    bf16, f32 = jnp.bfloat16, jnp.float32
    dma = pltpu.SemaphoreType.DMA
    return pl.pallas_call(
        kernel,
        out_shape=pltpu.VMEM((BLOCKS, ROWS, LAGS, CHAN), f32),
        in_specs=[
            pl.BlockSpec(memory_space=pltpu.SMEM),
            pl.BlockSpec(memory_space=pltpu.HBM),
            pl.BlockSpec(memory_space=pltpu.HBM),
            pl.BlockSpec(memory_space=pltpu.HBM),
        ],
        out_specs=pl.BlockSpec(memory_space=pltpu.VMEM),
        scratch_shapes=[
            pltpu.VMEM((1, CHAN), jnp.int32),
            pltpu.VMEM((FREQ, LAGS), f32),
            pltpu.VMEM((2, FREQ, CHAN), bf16),
            pltpu.VMEM((2, FREQ, CHAN), bf16),
            pltpu.VMEM((FREQ, CHAN), bf16),
            pltpu.VMEM((FREQ, CHAN), bf16),
            pltpu.VMEM((2, (N_Y - 1) * HALF, CHAN), bf16),
            pltpu.VMEM((2, HALF, CHAN), bf16),
            pltpu.VMEM((2, N_ZH - 1, HALF, CHAN), bf16),
            pltpu.VMEM((BLOCKS, 2 * FREQ, CHAN), bf16),
            pltpu.VMEM((2 * FREQ, WIDE), bf16),
            pltpu.VMEM((BLOCKS, 2, CHAN, SPAN), bf16),
            pltpu.VMEM((BLOCKS, 2, (SHOTS - 1) * ROWS, SPAN), bf16),
            pltpu.VMEM((BLOCKS, ROWS, LAGS, CHAN), f32),
            dma, dma, dma, dma, dma, dma((2,)), dma((2,)), dma((2,)), dma((2,)),
            pltpu.SemaphoreType.REGULAR((N_ZH,)), dma((2, N_ZH - 1)), dma((2, N_ZH - 1)), dma((2,)), dma((2,)),
            dma((4, 2, 4)), dma((4, 2, 4)),
            dma((BLOCKS,)), dma((BLOCKS,)), dma((BLOCKS, 2)), dma((BLOCKS, 2)),
        ],
        cost_estimate=pl.CostEstimate(flops=1_700_000_000, bytes_accessed=1_500_000, transcendentals=0),
        compiler_params=pltpu.CompilerParams(
            collective_id=0, has_side_effects=True, vmem_limit_bytes=62 * 2**20),
    )(owners, live_mask, jnp.asarray(lag_tables()), records.reshape(2, FREQ, CHAN))


def solution(mesh):
    in_specs = (P(None, "shot", None, "rcv"), P("shot", "rcv"), P())
    out_specs = P(None, "shot", None, "rcv")
    return jax.shard_map(
        on_device, mesh=mesh, in_specs=in_specs, out_specs=out_specs, check_vma=False
    )
```

```python
import functools
import math

import jax
import jax.numpy as jnp
import numpy as np
from jax import lax
from jax.experimental import pallas as pl
from jax.experimental.pallas import tpu as pltpu
from jax.sharding import PartitionSpec as P

FREQ = 1024
CHAN = 128
BLOCKS = 3
LAGS = 8
STRIDE = 16
N_ZH = 4
N_Y = 8
CHIPS = N_ZH * N_Y
N_RCV = 2 * CHIPS
SHOTS = 8
GROUP = FREQ // N_Y
MIDS = 1
HALF = GROUP // MIDS
ROWS = CHAN // SHOTS
WIDE = LAGS * CHAN
SPANS = 2
SPAN = WIDE // SPANS
MESH = pl.DeviceIdType.MESH


def lag_tables():
    f32 = np.float32
    freq_index = np.arange(FREQ, dtype=f32)
    lag_index = np.arange(LAGS, dtype=f32)
    shifts = (lag_index - f32(LAGS // 2)) * f32(STRIDE) + f32(STRIDE // 2)
    taper = f32(0.54) + f32(0.46) * np.cos(f32(2.0 * math.pi) * (lag_index + f32(0.5)) / f32(LAGS) - f32(math.pi))
    phases = f32(math.pi) * freq_index[:, None] * shifts[None, :] / f32(FREQ)
    weights = taper[None, :] / np.sqrt(f32(SHOTS * FREQ))
    half = LAGS // 2
    cos_table = (np.cos(phases) * weights)[:, :half]
    sin_table = (np.sin(phases) * weights)[:, :half]
    return np.concatenate([cos_table, sin_table], axis=1).astype(f32)


def kernel(
    owners_ref, mask_hbm, tab_hbm, rec_hbm, out_ref,
    mask_ref, tab_ref, rec, own, xb, ms, mr, mp, mz, pb, st, part, rb, acc, res,
    mask_sem, tab_sem, load_sem, sib_s, sib_r, scat_s, scat_r, mid_s, mid_r,
    mz_s, mz_r, z_s, z_r, y_s, y_r, d_s, d_r, rs_s, rs_r,
):
    r = lax.axis_index("rcv")
    s = lax.axis_index("shot")
    q = lax.div(r, 2)
    core = lax.rem(r, 2)
    zh = lax.div(q, N_Y)
    y = lax.rem(q, N_Y)
    sib = r + 1 - 2 * core

    def row_dev(d):
        return (zh * N_Y + lax.rem(y + d + N_Y, N_Y)) * 2 + core

    def column_dev(d):
        return (lax.rem(zh + d, N_ZH) * N_Y + y) * 2 + core

    def shot(d):
        return lax.rem(s + d, SHOTS)

    barrier = pltpu.get_barrier_semaphore()

    def greet(dev):
        pl.semaphore_signal(barrier, inc=1, device_id=dev, device_id_type=MESH)

    load = pltpu.make_async_copy(rec_hbm, rec, load_sem)
    load.start()
    load_mask = pltpu.make_async_copy(mask_hbm, mask_ref, mask_sem)
    load_mask.start()
    load_tab = pltpu.make_async_copy(tab_hbm, tab_ref, tab_sem)
    load_tab.start()
    for d in range(N_Y - 1, 0, -1):
        greet({"rcv": row_dev(d)})
    for d in range(1, N_ZH):
        greet({"rcv": column_dev(d)})
    greet({"rcv": sib})
    for d in range(1, SHOTS):
        greet({"shot": shot(d)})

    load.wait()

    def add_power(i, acc):
        rows = pl.ds(pl.multiple_of(i * 64, 64), 64)
        for p in range(2):
            v = rec[p, rows, :].astype(jnp.float32)
            v = v * v
            for j in range(8):
                acc = acc + v[8 * j:8 * j + 8]
        return acc

    total = lax.fori_loop(0, FREQ // 64, add_power, jnp.zeros((8, CHAN), jnp.float32))
    power = jnp.sum(total, axis=0, keepdims=True) * (1.0 / (2 * FREQ))
    load_mask.wait()
    gain = mask_ref[...].astype(jnp.float32) / jnp.sqrt(power + 1e-06)

    def whiten_part(p):
        def body(i, carry):
            rows = pl.ds(pl.multiple_of(i * 128, 128), 128)
            own[p, rows, :] = (rec[p, rows, :].astype(jnp.float32) * gain).astype(jnp.bfloat16)
            return carry
        lax.fori_loop(0, FREQ // 128, body, 0)

    whiten_part(1 - core)
    pl.semaphore_wait(barrier, N_Y - 1 + N_ZH - 1 + 1 + SHOTS - 1)
    swap = pltpu.make_async_remote_copy(
        src_ref=own.at[1 - core], dst_ref=xb, send_sem=sib_s, recv_sem=sib_r,
        device_id={"rcv": sib}, device_id_type=MESH)
    swap.start()
    whiten_part(core)
    swap.wait_recv()

    base = core * FREQ

    def rows_of(start, size):
        return pl.ds(pl.multiple_of(start, 16), size)

    my_rows = rows_of(base + y * GROUP, GROUP)

    def scatter(blk, src):
        for d in range(1, N_Y):
            row = lax.rem(y + d, N_Y) * GROUP
            pltpu.make_async_remote_copy(
                src_ref=src.at[rows_of(row, GROUP), :],
                dst_ref=pb.at[blk, rows_of(base + row, GROUP), :],
                send_sem=scat_s.at[blk], recv_sem=scat_r.at[blk],
                device_id={"rcv": row_dev(d)}, device_id_type=MESH).start()
        pb[blk, my_rows, :] = src[rows_of(y * GROUP, GROUP), :]

    @pl.when(r == 0)
    def _():
        scatter(0, own.at[0])

    @pl.when(r == 1)
    def _():
        scatter(0, xb)

    @pl.when(r == N_RCV - 1)
    def _():
        scatter(1, own.at[1])

    @pl.when(r == N_RCV - 2)
    def _():
        scatter(1, xb)

    mid = owners_ref[0] + owners_ref[1] + owners_ref[2] - (N_RCV - 1)
    is_me = jnp.where(mid == r, 1.0, 0.0).astype(jnp.float32)
    is_sib = jnp.where(mid == sib, 1.0, 0.0).astype(jnp.float32)

    def pick(i, carry):
        rows = pl.ds(pl.multiple_of(i * 128, 128), 128)
        mine = own[core, rows, :].astype(jnp.float32) * is_me
        other = xb[rows, :].astype(jnp.float32) * is_sib
        ms[rows, :] = (mine + other).astype(jnp.bfloat16)
        return carry

    lax.fori_loop(0, FREQ // 128, pick, 0)

    for h in range(MIDS):
        for d in (4, 3, 5, 2, 6, 1, 7):
            pltpu.make_async_remote_copy(
                src_ref=ms.at[rows_of(lax.rem(y + d, N_Y) * GROUP + h * HALF, HALF), :],
                dst_ref=mr.at[h, (d - 1) * HALF:d * HALF, :],
                send_sem=mid_s.at[h], recv_sem=mid_r.at[h],
                device_id={"rcv": row_dev(d)}, device_id_type=MESH).start()

    half = LAGS // 2

    def steer(i, carry):
        rows = pl.ds(pl.multiple_of(i * 16, 16), 16)
        low = pl.ds(pl.multiple_of(FREQ + i * 16, 16), 16)
        a = rec[0, rows, :].astype(jnp.float32) * gain
        b = rec[1, rows, :].astype(jnp.float32) * gain
        for l in range(half):
            c = jnp.broadcast_to(tab_ref[rows, l:l + 1], (16, CHAN))
            t = jnp.broadcast_to(tab_ref[rows, half + l:half + l + 1], (16, CHAN))
            ac, bt, at, bc = a * c, b * t, a * t, b * c
            near = slice(l * CHAN, (l + 1) * CHAN)
            far = slice((LAGS - 1 - l) * CHAN, (LAGS - l) * CHAN)
            st[rows, near] = (ac - bt).astype(jnp.bfloat16)
            st[rows, far] = (ac + bt).astype(jnp.bfloat16)
            st[low, near] = (at + bc).astype(jnp.bfloat16)
            st[low, far] = (bc - at).astype(jnp.bfloat16)
        return carry

    load_tab.wait()
    lax.fori_loop(0, FREQ // 16, steer, 0)

    def wait_rows(ref, sem):
        pltpu.make_async_copy(ref, ref, sem).wait()

    def column_send(blk):
        for z2 in range(N_ZH):
            @pl.when(zh != z2)
            def _():
                pltpu.make_async_remote_copy(
                    src_ref=pb.at[blk, my_rows, :], dst_ref=pb.at[blk, my_rows, :],
                    send_sem=z_s.at[blk], recv_sem=z_r.at[blk],
                    device_id={"rcv": (z2 * N_Y + y) * 2 + core}, device_id_type=MESH).start()

    def mid_copy(h, d):
        return pltpu.make_async_remote_copy(
            src_ref=mp.at[h], dst_ref=mz.at[h, d - 1],
            send_sem=mz_s.at[h, d - 1], recv_sem=mz_r.at[h, d - 1],
            device_id={"rcv": column_dev(d)}, device_id_type=MESH)

    def mid_row(h):
        wait_rows(mr.at[h], mid_r.at[h])
        acc = ms[rows_of(y * GROUP + h * HALF, HALF), :]
        for d in range(N_Y - 1):
            acc = acc + mr[h, d * HALF:(d + 1) * HALF, :]
        mp[h] = acc
        for z2 in range(N_ZH):
            @pl.when(zh != z2)
            def _():
                mid_copy(h, lax.rem(z2 - zh + N_ZH, N_ZH)).start()

    def mid_column(h):
        acc = mp[h]
        for d in range(1, N_ZH):
            mid_copy(h, d).wait_recv()
            acc = acc + mz[h, d - 1]
        pb[2, rows_of(base + y * GROUP + h * HALF, HALF), :] = acc

    def ring_at(offset):
        return lax.rem(y + N_Y + offset, N_Y)

    def ring_rows(part_set, offset, way, j):
        _, low, size, _ = part_set
        start = base + ring_at(offset) * GROUP + low
        if j < 3:
            return rows_of(start, size)
        return rows_of(start + way * (size // 2), size // 2)

    def ring_copy(part_set, way, j):
        blk, _, _, at = part_set
        sign = -1 if way else 1
        rows = ring_rows(part_set, 0 if j < 2 else -2 * sign, way, j)
        return pltpu.make_async_remote_copy(
            src_ref=pb.at[blk, rows, :], dst_ref=pb.at[blk, rows, :],
            send_sem=y_s.at[at, way, j], recv_sem=y_r.at[at, way, j],
            device_id={"rcv": row_dev((2, 1, 1, 2)[j] * sign)}, device_id_type=MESH)

    def to_sibling(blk, rows):
        pltpu.make_async_remote_copy(
            src_ref=pb.at[blk, rows, :], dst_ref=pb.at[blk, rows, :],
            send_sem=d_s.at[blk], recv_sem=d_r.at[blk],
            device_id={"rcv": sib}, device_id_type=MESH).start()

    def ring_recv(part_set, j):
        for way in range(2):
            sign = -1 if way else 1
            ring_copy(part_set, way, j).wait_recv()
            if j == 0:
                ring_copy(part_set, way, 2).start()
                ring_copy(part_set, way, 3).start()
        for way in range(2):
            sign = -1 if way else 1
            to_sibling(part_set[0], ring_rows(part_set, -(2, 1, 3, 4)[j] * sign, way, j))

    def ring_start(part_set):
        for j in range(2):
            for way in range(2):
                ring_copy(part_set, way, j).start()
        to_sibling(part_set[0], ring_rows(part_set, 0, 0, 0))

    def correlate(blk):
        def product(rows, cols):
            return lax.dot_general(
                pb[blk, rows, :], st[rows, cols], (((0,), (0,)), ((), ())),
                preferred_element_type=jnp.float32)

        quarters = [slice(n * 256, (n + 1) * 256) for n in range(4)]
        for cols in quarters:
            acc[:, cols] = product(pl.ds(pl.multiple_of(base, FREQ), FREQ), cols)
        wait_rows(pb.at[blk, pl.ds(0, FREQ), :], d_r.at[blk])
        for half_span in range(SPANS):
            for n in range(4 // SPANS):
                cols = quarters[half_span * (4 // SPANS) + n]
                both = acc[:, cols] + product(pl.ds(pl.multiple_of(FREQ - base, FREQ), FREQ), cols)
                part[blk, half_span, :, n * 256:(n + 1) * 256] = both.astype(jnp.bfloat16)
            for d in (4, 5, 3, 6, 2, 1, 7):
                s2 = shot(d)
                pltpu.make_async_remote_copy(
                    src_ref=part.at[blk, half_span, pl.ds(pl.multiple_of(s2 * ROWS, ROWS), ROWS), :],
                    dst_ref=rb.at[blk, half_span, (d - 1) * ROWS:d * ROWS, :],
                    send_sem=rs_s.at[blk, half_span], recv_sem=rs_r.at[blk, half_span],
                    device_id={"shot": s2}, device_id_type=MESH).start()

    def stack(blk):
        mine = pl.ds(pl.multiple_of(s * ROWS, ROWS), ROWS)
        for l in range(LAGS):
            half_span, n = l // (LAGS // SPANS), l % (LAGS // SPANS)
            if n == 0:
                wait_rows(rb.at[blk, half_span], rs_r.at[blk, half_span])
            cols = slice(n * CHAN, (n + 1) * CHAN)
            total = part[blk, half_span, mine, cols].astype(jnp.float32)
            for d in range(SHOTS - 1):
                total = total + rb[blk, half_span, d * ROWS:(d + 1) * ROWS, cols].astype(jnp.float32)
            res[blk, :, l, :] = total

    for blk, root in ((0, 0), (1, CHIPS - 1)):
        @pl.when(zh == root // N_Y)
        def _():
            @pl.when(y != root % N_Y)
            def _():
                wait_rows(pb.at[blk, my_rows, :], scat_r.at[blk])
            column_send(blk)

    for h in range(MIDS):
        mid_row(h)

    sets = [(0, 0, GROUP, 0), (1, 0, GROUP, 1)]
    sets = sets + [(2, h * HALF, HALF, 2 + h) for h in range(MIDS)]
    for blk, root in ((0, 0), (1, CHIPS - 1)):
        @pl.when(zh != root // N_Y)
        def _():
            wait_rows(pb.at[blk, my_rows, :], z_r.at[blk])
        ring_start(sets[blk])
    for h in range(MIDS):
        mid_column(h)
        ring_start(sets[2 + h])
    for part_set in sets:
        ring_recv(part_set, 0)
    def ring_rest(blk):
        for part_set in sets:
            if part_set[0] == blk:
                for j in range(1, 4):
                    ring_recv(part_set, j)

    ring_rest(0)
    ring_rest(1)
    correlate(0)
    ring_rest(2)
    correlate(1)
    correlate(2)
    for blk in range(BLOCKS):
        stack(blk)

    for b in range(BLOCKS):
        owner = jnp.full((ROWS, LAGS, CHAN), owners_ref[b], jnp.int32)
        out_ref[b] = jnp.where(owner == 0, res[0], jnp.where(owner == N_RCV - 1, res[1], res[2]))

    swap.wait_send()
    for h in range(MIDS):
        wait_rows(mr.at[h], mid_s.at[h])
        for d in range(1, N_ZH):
            mid_copy(h, d).wait_send()
    for blk, root in ((0, 0), (1, CHIPS - 1)):
        @pl.when(q == root)
        def _():
            wait_rows(pb.at[blk, pl.ds(0, FREQ - GROUP), :], scat_s.at[blk])

        @pl.when(zh == root // N_Y)
        def _():
            wait_rows(pb.at[blk, pl.ds(0, (N_ZH - 1) * GROUP), :], z_s.at[blk])
    for part_set in sets:
        for j in range(4):
            for way in range(2):
                ring_copy(part_set, way, j).wait_send()
    for blk in range(BLOCKS):
        wait_rows(pb.at[blk, pl.ds(0, FREQ), :], d_s.at[blk])
        for half_span in range(SPANS):
            wait_rows(rb.at[blk, half_span], rs_s.at[blk, half_span])


def on_device(records, live_mask, owners):
    bf16, f32 = jnp.bfloat16, jnp.float32
    dma = pltpu.SemaphoreType.DMA
    return pl.pallas_call(
        kernel,
        out_shape=pltpu.VMEM((BLOCKS, ROWS, LAGS, CHAN), f32),
        in_specs=[
            pl.BlockSpec(memory_space=pltpu.SMEM),
            pl.BlockSpec(memory_space=pltpu.HBM),
            pl.BlockSpec(memory_space=pltpu.HBM),
            pl.BlockSpec(memory_space=pltpu.HBM),
        ],
        out_specs=pl.BlockSpec(memory_space=pltpu.VMEM),
        scratch_shapes=[
            pltpu.VMEM((1, CHAN), jnp.int32),
            pltpu.VMEM((FREQ, LAGS), f32),
            pltpu.VMEM((2, FREQ, CHAN), bf16),
            pltpu.VMEM((2, FREQ, CHAN), bf16),
            pltpu.VMEM((FREQ, CHAN), bf16),
            pltpu.VMEM((FREQ, CHAN), bf16),
            pltpu.VMEM((MIDS, (N_Y - 1) * HALF, CHAN), bf16),
            pltpu.VMEM((MIDS, HALF, CHAN), bf16),
            pltpu.VMEM((MIDS, N_ZH - 1, HALF, CHAN), bf16),
            pltpu.VMEM((BLOCKS, 2 * FREQ, CHAN), bf16),
            pltpu.VMEM((2 * FREQ, WIDE), bf16),
            pltpu.VMEM((BLOCKS, SPANS, CHAN, SPAN), bf16),
            pltpu.VMEM((BLOCKS, SPANS, (SHOTS - 1) * ROWS, SPAN), bf16),
            pltpu.VMEM((CHAN, WIDE), f32),
            pltpu.VMEM((BLOCKS, ROWS, LAGS, CHAN), f32),
            dma, dma, dma, dma, dma, dma((2,)), dma((2,)), dma((2,)), dma((2,)),
            dma((2, N_ZH - 1)), dma((2, N_ZH - 1)), dma((2,)), dma((2,)),
            dma((4, 2, 4)), dma((4, 2, 4)),
            dma((BLOCKS,)), dma((BLOCKS,)), dma((BLOCKS, 2)), dma((BLOCKS, 2)),
        ],
        cost_estimate=pl.CostEstimate(flops=1_700_000_000, bytes_accessed=1_500_000, transcendentals=0),
        compiler_params=pltpu.CompilerParams(
            collective_id=0, has_side_effects=True, vmem_limit_bytes=62 * 2**20),
    )(owners, live_mask, jnp.asarray(lag_tables()), records.reshape(2, FREQ, CHAN))


def solution(mesh):
    in_specs = (P(None, "shot", None, "rcv"), P("shot", "rcv"), P())
    out_specs = P(None, "shot", None, "rcv")
    return jax.shard_map(
        on_device, mesh=mesh, in_specs=in_specs, out_specs=out_specs, check_vma=False
    )
```

```python
import functools
import math

import jax
import jax.numpy as jnp
import numpy as np
from jax import lax
from jax.experimental import pallas as pl
from jax.experimental.pallas import tpu as pltpu
from jax.sharding import PartitionSpec as P

FREQ = 1024
CHAN = 128
BLOCKS = 3
LAGS = 8
STRIDE = 16
N_ZH = 4
N_Y = 8
CHIPS = N_ZH * N_Y
N_RCV = 2 * CHIPS
SHOTS = 8
GROUP = FREQ // N_Y
MIDS = 1
HALF = GROUP // MIDS
ROWS = CHAN // SHOTS
WIDE = LAGS * CHAN
SPANS = 2
SPAN = WIDE // SPANS
MESH = pl.DeviceIdType.MESH


def lag_tables():
    f32 = np.float32
    freq_index = np.arange(FREQ, dtype=f32)
    lag_index = np.arange(LAGS, dtype=f32)
    shifts = (lag_index - f32(LAGS // 2)) * f32(STRIDE) + f32(STRIDE // 2)
    taper = f32(0.54) + f32(0.46) * np.cos(f32(2.0 * math.pi) * (lag_index + f32(0.5)) / f32(LAGS) - f32(math.pi))
    phases = f32(math.pi) * freq_index[:, None] * shifts[None, :] / f32(FREQ)
    weights = taper[None, :] / np.sqrt(f32(SHOTS * FREQ))
    half = LAGS // 2
    cos_table = (np.cos(phases) * weights)[:, :half]
    sin_table = (np.sin(phases) * weights)[:, :half]
    return np.concatenate([cos_table, sin_table], axis=1).astype(f32)


def kernel(
    owners_ref, mask_hbm, tab_hbm, rec_hbm, out_ref,
    mask_ref, tab_ref, rec, own, xb, ms, mr, mp, mz, pb, st, part, rb, acc, res,
    mask_sem, tab_sem, load_sem, sib_s, sib_r, scat_s, scat_r, mid_s, mid_r,
    mz_s, mz_r, z_s, z_r, y_s, y_r, d_s, d_r, rs_s, rs_r,
):
    r = lax.axis_index("rcv")
    s = lax.axis_index("shot")
    q = lax.div(r, 2)
    core = lax.rem(r, 2)
    zh = lax.div(q, N_Y)
    y = lax.rem(q, N_Y)
    sib = r + 1 - 2 * core

    def row_dev(d):
        return (zh * N_Y + lax.rem(y + d + N_Y, N_Y)) * 2 + core

    def column_dev(d):
        return (lax.rem(zh + d, N_ZH) * N_Y + y) * 2 + core

    def shot(d):
        return lax.rem(s + d, SHOTS)

    barrier = pltpu.get_barrier_semaphore()

    def greet(dev):
        pl.semaphore_signal(barrier, inc=1, device_id=dev, device_id_type=MESH)

    load = pltpu.make_async_copy(rec_hbm, rec, load_sem)
    load.start()
    load_mask = pltpu.make_async_copy(mask_hbm, mask_ref, mask_sem)
    load_mask.start()
    load_tab = pltpu.make_async_copy(tab_hbm, tab_ref, tab_sem)
    load_tab.start()
    for d in range(N_Y - 1, 0, -1):
        greet({"rcv": row_dev(d)})
    for d in range(1, N_ZH):
        greet({"rcv": column_dev(d)})
    greet({"rcv": sib})
    for d in range(1, SHOTS):
        greet({"shot": shot(d)})

    load.wait()

    def add_power(i, acc):
        rows = pl.ds(pl.multiple_of(i * 64, 64), 64)
        for p in range(2):
            v = rec[p, rows, :].astype(jnp.float32)
            v = v * v
            for j in range(8):
                acc = acc + v[8 * j:8 * j + 8]
        return acc

    total = lax.fori_loop(0, FREQ // 64, add_power, jnp.zeros((8, CHAN), jnp.float32))
    power = jnp.sum(total, axis=0, keepdims=True) * (1.0 / (2 * FREQ))
    load_mask.wait()
    gain = mask_ref[...].astype(jnp.float32) / jnp.sqrt(power + 1e-06)

    def whiten_part(p):
        def body(i, carry):
            rows = pl.ds(pl.multiple_of(i * 128, 128), 128)
            own[p, rows, :] = (rec[p, rows, :].astype(jnp.float32) * gain).astype(jnp.bfloat16)
            return carry
        lax.fori_loop(0, FREQ // 128, body, 0)

    whiten_part(1 - core)
    pl.semaphore_wait(barrier, N_Y - 1 + N_ZH - 1 + 1 + SHOTS - 1)
    swap = pltpu.make_async_remote_copy(
        src_ref=own.at[1 - core], dst_ref=xb, send_sem=sib_s, recv_sem=sib_r,
        device_id={"rcv": sib}, device_id_type=MESH)
    swap.start()
    whiten_part(core)
    swap.wait_recv()

    base = core * FREQ

    def rows_of(start, size):
        return pl.ds(pl.multiple_of(start, 16), size)

    my_rows = rows_of(base + y * GROUP, GROUP)

    def scatter(blk, src):
        for d in range(1, N_Y):
            row = lax.rem(y + d, N_Y) * GROUP
            pltpu.make_async_remote_copy(
                src_ref=src.at[rows_of(row, GROUP), :],
                dst_ref=pb.at[blk, rows_of(base + row, GROUP), :],
                send_sem=scat_s.at[blk], recv_sem=scat_r.at[blk],
                device_id={"rcv": row_dev(d)}, device_id_type=MESH).start()
        pb[blk, my_rows, :] = src[rows_of(y * GROUP, GROUP), :]

    @pl.when(r == 0)
    def _():
        scatter(0, own.at[0])

    @pl.when(r == 1)
    def _():
        scatter(0, xb)

    @pl.when(r == N_RCV - 1)
    def _():
        scatter(1, own.at[1])

    @pl.when(r == N_RCV - 2)
    def _():
        scatter(1, xb)

    mid = owners_ref[0] + owners_ref[1] + owners_ref[2] - (N_RCV - 1)
    is_me = jnp.where(mid == r, 1.0, 0.0).astype(jnp.float32)
    is_sib = jnp.where(mid == sib, 1.0, 0.0).astype(jnp.float32)

    def pick(i, carry):
        rows = pl.ds(pl.multiple_of(i * 128, 128), 128)
        mine = own[core, rows, :].astype(jnp.float32) * is_me
        other = xb[rows, :].astype(jnp.float32) * is_sib
        ms[rows, :] = (mine + other).astype(jnp.bfloat16)
        return carry

    lax.fori_loop(0, FREQ // 128, pick, 0)

    for h in range(MIDS):
        for d in (4, 3, 5, 2, 6, 1, 7):
            pltpu.make_async_remote_copy(
                src_ref=ms.at[rows_of(lax.rem(y + d, N_Y) * GROUP + h * HALF, HALF), :],
                dst_ref=mr.at[h, (d - 1) * HALF:d * HALF, :],
                send_sem=mid_s.at[h], recv_sem=mid_r.at[h],
                device_id={"rcv": row_dev(d)}, device_id_type=MESH).start()

    half = LAGS // 2

    def steer(i, carry):
        rows = pl.ds(pl.multiple_of(i * 16, 16), 16)
        low = pl.ds(pl.multiple_of(FREQ + i * 16, 16), 16)
        a = rec[0, rows, :].astype(jnp.float32) * gain
        b = rec[1, rows, :].astype(jnp.float32) * gain
        for l in range(half):
            c = jnp.broadcast_to(tab_ref[rows, l:l + 1], (16, CHAN))
            t = jnp.broadcast_to(tab_ref[rows, half + l:half + l + 1], (16, CHAN))
            ac, bt, at, bc = a * c, b * t, a * t, b * c
            near = slice(l * CHAN, (l + 1) * CHAN)
            far = slice((LAGS - 1 - l) * CHAN, (LAGS - l) * CHAN)
            st[rows, near] = (ac - bt).astype(jnp.bfloat16)
            st[rows, far] = (ac + bt).astype(jnp.bfloat16)
            st[low, near] = (at + bc).astype(jnp.bfloat16)
            st[low, far] = (bc - at).astype(jnp.bfloat16)
        return carry

    load_tab.wait()
    lax.fori_loop(0, FREQ // 16, steer, 0)

    def wait_rows(ref, sem):
        pltpu.make_async_copy(ref, ref, sem).wait()

    def column_send(blk):
        for z2 in range(N_ZH):
            @pl.when(zh != z2)
            def _():
                pltpu.make_async_remote_copy(
                    src_ref=pb.at[blk, my_rows, :], dst_ref=pb.at[blk, my_rows, :],
                    send_sem=z_s.at[blk], recv_sem=z_r.at[blk],
                    device_id={"rcv": (z2 * N_Y + y) * 2 + core}, device_id_type=MESH).start()

    def mid_copy(h, d):
        return pltpu.make_async_remote_copy(
            src_ref=mp.at[h], dst_ref=mz.at[h, d - 1],
            send_sem=mz_s.at[h, d - 1], recv_sem=mz_r.at[h, d - 1],
            device_id={"rcv": column_dev(d)}, device_id_type=MESH)

    def mid_row(h):
        wait_rows(mr.at[h], mid_r.at[h])
        acc = ms[rows_of(y * GROUP + h * HALF, HALF), :]
        for d in range(N_Y - 1):
            acc = acc + mr[h, d * HALF:(d + 1) * HALF, :]
        mp[h] = acc
        for z2 in range(N_ZH):
            @pl.when(zh != z2)
            def _():
                mid_copy(h, lax.rem(z2 - zh + N_ZH, N_ZH)).start()

    def mid_column(h):
        acc = mp[h]
        for d in range(1, N_ZH):
            mid_copy(h, d).wait_recv()
            acc = acc + mz[h, d - 1]
        pb[2, rows_of(base + y * GROUP + h * HALF, HALF), :] = acc

    def ring_at(offset):
        return lax.rem(y + N_Y + offset, N_Y)

    def ring_rows(part_set, offset, way, j):
        _, low, size, _ = part_set
        start = base + ring_at(offset) * GROUP + low
        if j < 3:
            return rows_of(start, size)
        return rows_of(start + way * (size // 2), size // 2)

    def ring_copy(part_set, way, j):
        blk, _, _, at = part_set
        sign = -1 if way else 1
        rows = ring_rows(part_set, 0 if j < 2 else -2 * sign, way, j)
        return pltpu.make_async_remote_copy(
            src_ref=pb.at[blk, rows, :], dst_ref=pb.at[blk, rows, :],
            send_sem=y_s.at[at, way, j], recv_sem=y_r.at[at, way, j],
            device_id={"rcv": row_dev((2, 1, 1, 2)[j] * sign)}, device_id_type=MESH)

    def to_sibling(blk, rows):
        pltpu.make_async_remote_copy(
            src_ref=pb.at[blk, rows, :], dst_ref=pb.at[blk, rows, :],
            send_sem=d_s.at[blk], recv_sem=d_r.at[blk],
            device_id={"rcv": sib}, device_id_type=MESH).start()

    def ring_recv(part_set, j):
        for way in range(2):
            sign = -1 if way else 1
            ring_copy(part_set, way, j).wait_recv()
            if j == 0:
                ring_copy(part_set, way, 2).start()
                ring_copy(part_set, way, 3).start()
        for way in range(2):
            sign = -1 if way else 1
            to_sibling(part_set[0], ring_rows(part_set, -(2, 1, 3, 4)[j] * sign, way, j))

    def ring_start(part_set):
        for j in range(2):
            for way in range(2):
                ring_copy(part_set, way, j).start()
        to_sibling(part_set[0], ring_rows(part_set, 0, 0, 0))

    def correlate(blk):
        def product(rows, cols):
            return lax.dot_general(
                pb[blk, rows, :], st[rows, cols], (((0,), (0,)), ((), ())),
                preferred_element_type=jnp.float32)

        quarters = [slice(n * 256, (n + 1) * 256) for n in range(4)]
        for cols in quarters:
            acc[:, cols] = product(pl.ds(pl.multiple_of(base, FREQ), FREQ), cols)
        wait_rows(pb.at[blk, pl.ds(0, FREQ), :], d_r.at[blk])
        for half_span in range(SPANS):
            for n in range(4 // SPANS):
                cols = quarters[half_span * (4 // SPANS) + n]
                both = acc[:, cols] + product(pl.ds(pl.multiple_of(FREQ - base, FREQ), FREQ), cols)
                part[blk, half_span, :, n * 256:(n + 1) * 256] = both.astype(jnp.bfloat16)
            for d in (4, 5, 3, 6, 2, 1, 7):
                s2 = shot(d)
                pltpu.make_async_remote_copy(
                    src_ref=part.at[blk, half_span, pl.ds(pl.multiple_of(s2 * ROWS, ROWS), ROWS), :],
                    dst_ref=rb.at[blk, half_span, (d - 1) * ROWS:d * ROWS, :],
                    send_sem=rs_s.at[blk, half_span], recv_sem=rs_r.at[blk, half_span],
                    device_id={"shot": s2}, device_id_type=MESH).start()

    def stack(blk):
        mine = pl.ds(pl.multiple_of(s * ROWS, ROWS), ROWS)
        for l in range(LAGS):
            half_span, n = l // (LAGS // SPANS), l % (LAGS // SPANS)
            if n == 0:
                wait_rows(rb.at[blk, half_span], rs_r.at[blk, half_span])
            cols = slice(n * CHAN, (n + 1) * CHAN)
            total = part[blk, half_span, mine, cols].astype(jnp.float32)
            for d in range(SHOTS - 1):
                total = total + rb[blk, half_span, d * ROWS:(d + 1) * ROWS, cols].astype(jnp.float32)
            res[blk, :, l, :] = total

    for blk, root in ((0, 0), (1, CHIPS - 1)):
        @pl.when(zh == root // N_Y)
        def _():
            @pl.when(y != root % N_Y)
            def _():
                wait_rows(pb.at[blk, my_rows, :], scat_r.at[blk])
            column_send(blk)

    for h in range(MIDS):
        mid_row(h)

    sets = [(0, 0, GROUP, 0), (1, 0, GROUP, 1)]
    sets = sets + [(2, h * HALF, HALF, 2 + h) for h in range(MIDS)]
    for blk, root in ((0, 0), (1, CHIPS - 1)):
        @pl.when(zh != root // N_Y)
        def _():
            wait_rows(pb.at[blk, my_rows, :], z_r.at[blk])
        ring_start(sets[blk])
    ring_recv(sets[0], 0)
    for h in range(MIDS):
        mid_column(h)
        ring_start(sets[2 + h])
    ring_recv(sets[1], 0)
    ring_recv(sets[2], 0)

    def ring_rest(blk):
        for part_set in sets:
            if part_set[0] == blk:
                for j in range(1, 4):
                    ring_recv(part_set, j)

    ring_rest(0)
    ring_rest(1)
    correlate(0)
    ring_rest(2)
    correlate(1)
    correlate(2)
    swap.wait_send()
    for h in range(MIDS):
        wait_rows(mr.at[h], mid_s.at[h])
        for d in range(1, N_ZH):
            mid_copy(h, d).wait_send()
    for blk, root in ((0, 0), (1, CHIPS - 1)):
        @pl.when(q == root)
        def _():
            wait_rows(pb.at[blk, pl.ds(0, FREQ - GROUP), :], scat_s.at[blk])

        @pl.when(zh == root // N_Y)
        def _():
            wait_rows(pb.at[blk, pl.ds(0, (N_ZH - 1) * GROUP), :], z_s.at[blk])
    for part_set in sets:
        for j in range(4):
            for way in range(2):
                ring_copy(part_set, way, j).wait_send()
    for blk in range(BLOCKS):
        wait_rows(pb.at[blk, pl.ds(0, FREQ), :], d_s.at[blk])

    for blk in range(BLOCKS):
        stack(blk)

    for b in range(BLOCKS):
        owner = jnp.full((ROWS, LAGS, CHAN), owners_ref[b], jnp.int32)
        out_ref[b] = jnp.where(owner == 0, res[0], jnp.where(owner == N_RCV - 1, res[1], res[2]))

    for blk in range(BLOCKS):
        for half_span in range(SPANS):
            wait_rows(rb.at[blk, half_span], rs_s.at[blk, half_span])


def on_device(records, live_mask, owners):
    bf16, f32 = jnp.bfloat16, jnp.float32
    dma = pltpu.SemaphoreType.DMA
    return pl.pallas_call(
        kernel,
        out_shape=pltpu.VMEM((BLOCKS, ROWS, LAGS, CHAN), f32),
        in_specs=[
            pl.BlockSpec(memory_space=pltpu.SMEM),
            pl.BlockSpec(memory_space=pltpu.HBM),
            pl.BlockSpec(memory_space=pltpu.HBM),
            pl.BlockSpec(memory_space=pltpu.HBM),
        ],
        out_specs=pl.BlockSpec(memory_space=pltpu.VMEM),
        scratch_shapes=[
            pltpu.VMEM((1, CHAN), jnp.int32),
            pltpu.VMEM((FREQ, LAGS), f32),
            pltpu.VMEM((2, FREQ, CHAN), bf16),
            pltpu.VMEM((2, FREQ, CHAN), bf16),
            pltpu.VMEM((FREQ, CHAN), bf16),
            pltpu.VMEM((FREQ, CHAN), bf16),
            pltpu.VMEM((MIDS, (N_Y - 1) * HALF, CHAN), bf16),
            pltpu.VMEM((MIDS, HALF, CHAN), bf16),
            pltpu.VMEM((MIDS, N_ZH - 1, HALF, CHAN), bf16),
            pltpu.VMEM((BLOCKS, 2 * FREQ, CHAN), bf16),
            pltpu.VMEM((2 * FREQ, WIDE), bf16),
            pltpu.VMEM((BLOCKS, SPANS, CHAN, SPAN), bf16),
            pltpu.VMEM((BLOCKS, SPANS, (SHOTS - 1) * ROWS, SPAN), bf16),
            pltpu.VMEM((CHAN, WIDE), f32),
            pltpu.VMEM((BLOCKS, ROWS, LAGS, CHAN), f32),
            dma, dma, dma, dma, dma, dma((2,)), dma((2,)), dma((2,)), dma((2,)),
            dma((2, N_ZH - 1)), dma((2, N_ZH - 1)), dma((2,)), dma((2,)),
            dma((4, 2, 4)), dma((4, 2, 4)),
            dma((BLOCKS,)), dma((BLOCKS,)), dma((BLOCKS, 2)), dma((BLOCKS, 2)),
        ],
        cost_estimate=pl.CostEstimate(flops=1_700_000_000, bytes_accessed=1_500_000, transcendentals=0),
        compiler_params=pltpu.CompilerParams(
            collective_id=0, has_side_effects=True, vmem_limit_bytes=62 * 2**20),
    )(owners, live_mask, jnp.asarray(lag_tables()), records.reshape(2, FREQ, CHAN))


def solution(mesh):
    in_specs = (P(None, "shot", None, "rcv"), P("shot", "rcv"), P())
    out_specs = P(None, "shot", None, "rcv")
    return jax.shard_map(
        on_device, mesh=mesh, in_specs=in_specs, out_specs=out_specs, check_vma=False
    )
```

```python
import functools
import math

import jax
import jax.numpy as jnp
import numpy as np
from jax import lax
from jax.experimental import pallas as pl
from jax.experimental.pallas import tpu as pltpu
from jax.sharding import PartitionSpec as P

FREQ = 1024
CHAN = 128
BLOCKS = 3
LAGS = 8
STRIDE = 16
N_ZH = 4
N_Y = 8
CHIPS = N_ZH * N_Y
N_RCV = 2 * CHIPS
SHOTS = 8
GROUP = FREQ // N_Y
MIDS = 1
WHOLE = (0, 1, 2)
HALF = GROUP // MIDS
ROWS = CHAN // SHOTS
WIDE = LAGS * CHAN
SPANS = 2
SPAN = WIDE // SPANS
MESH = pl.DeviceIdType.MESH


def lag_tables():
    f32 = np.float32
    freq_index = np.arange(FREQ, dtype=f32)
    lag_index = np.arange(LAGS, dtype=f32)
    shifts = (lag_index - f32(LAGS // 2)) * f32(STRIDE) + f32(STRIDE // 2)
    taper = f32(0.54) + f32(0.46) * np.cos(f32(2.0 * math.pi) * (lag_index + f32(0.5)) / f32(LAGS) - f32(math.pi))
    phases = f32(math.pi) * freq_index[:, None] * shifts[None, :] / f32(FREQ)
    weights = taper[None, :] / np.sqrt(f32(SHOTS * FREQ))
    half = LAGS // 2
    cos_table = (np.cos(phases) * weights)[:, :half]
    sin_table = (np.sin(phases) * weights)[:, :half]
    return np.concatenate([cos_table, sin_table], axis=1).astype(f32)


def kernel(
    owners_ref, mask_hbm, tab_hbm, rec_hbm, out_ref,
    mask_ref, tab_ref, rec, own, xb, ms, mr, mp, mz, pb, st, part, rb, acc, res,
    mask_sem, tab_sem, load_sem, sib_s, sib_r, scat_s, scat_r, mid_s, mid_r,
    ready, mz_s, mz_r, z_s, z_r, y_s, y_r, d_s, d_r, rs_s, rs_r,
):
    r = lax.axis_index("rcv")
    s = lax.axis_index("shot")
    q = lax.div(r, 2)
    core = lax.rem(r, 2)
    zh = lax.div(q, N_Y)
    y = lax.rem(q, N_Y)
    sib = r + 1 - 2 * core

    def row_dev(d):
        return (zh * N_Y + lax.rem(y + d + N_Y, N_Y)) * 2 + core

    def column_dev(d):
        return (lax.rem(zh + d, N_ZH) * N_Y + y) * 2 + core

    def row_z(z2):
        return (z2 * N_Y + y) * 2 + core

    def shot(d):
        return lax.rem(s + d, SHOTS)

    barrier = pltpu.get_barrier_semaphore()

    def greet(dev):
        pl.semaphore_signal(barrier, inc=1, device_id=dev, device_id_type=MESH)

    load = pltpu.make_async_copy(rec_hbm, rec, load_sem)
    load.start()
    load_mask = pltpu.make_async_copy(mask_hbm, mask_ref, mask_sem)
    load_mask.start()
    load_tab = pltpu.make_async_copy(tab_hbm, tab_ref, tab_sem)
    load_tab.start()
    for d in range(N_Y - 1, 0, -1):
        greet({"rcv": row_dev(d)})
    for z2 in range(1, N_ZH):
        @pl.when(zh < z2)
        def _():
            greet({"rcv": row_z(z2)})
    greet({"rcv": sib})
    for d in range(1, SHOTS):
        greet({"shot": shot(d)})

    load.wait()

    def add_power(i, acc):
        rows = pl.ds(pl.multiple_of(i * 64, 64), 64)
        for p in range(2):
            v = rec[p, rows, :].astype(jnp.float32)
            v = v * v
            for j in range(8):
                acc = acc + v[8 * j:8 * j + 8]
        return acc

    total = lax.fori_loop(0, FREQ // 64, add_power, jnp.zeros((8, CHAN), jnp.float32))
    power = jnp.sum(total, axis=0, keepdims=True) * (1.0 / (2 * FREQ))
    load_mask.wait()
    gain = mask_ref[...].astype(jnp.float32) / jnp.sqrt(power + 1e-06)

    def whiten_part(p):
        def body(i, carry):
            rows = pl.ds(pl.multiple_of(i * 128, 128), 128)
            own[p, rows, :] = (rec[p, rows, :].astype(jnp.float32) * gain).astype(jnp.bfloat16)
            return carry
        lax.fori_loop(0, FREQ // 128, body, 0)

    whiten_part(1 - core)
    pl.semaphore_wait(barrier, N_Y - 1 + zh + 1 + SHOTS - 1)
    swap = pltpu.make_async_remote_copy(
        src_ref=own.at[1 - core], dst_ref=xb, send_sem=sib_s, recv_sem=sib_r,
        device_id={"rcv": sib}, device_id_type=MESH)
    swap.start()
    for z2 in range(N_ZH - 1):
        @pl.when(zh > z2)
        def _():
            pl.semaphore_signal(ready.at[zh], inc=1, device_id={"rcv": row_z(z2)}, device_id_type=MESH)

    whiten_part(core)
    swap.wait_recv()

    base = core * FREQ

    def rows_of(start, size):
        return pl.ds(pl.multiple_of(start, 16), size)

    my_rows = rows_of(base + y * GROUP, GROUP)

    def scatter(blk, src):
        for d in range(1, N_Y):
            row = lax.rem(y + d, N_Y) * GROUP
            pltpu.make_async_remote_copy(
                src_ref=src.at[rows_of(row, GROUP), :],
                dst_ref=pb.at[blk, rows_of(base + row, GROUP), :],
                send_sem=scat_s.at[blk], recv_sem=scat_r.at[blk],
                device_id={"rcv": row_dev(d)}, device_id_type=MESH).start()
        pb[blk, my_rows, :] = src[rows_of(y * GROUP, GROUP), :]

    @pl.when(r == 0)
    def _():
        scatter(0, own.at[0])

    @pl.when(r == 1)
    def _():
        scatter(0, xb)

    @pl.when(r == N_RCV - 1)
    def _():
        scatter(1, own.at[1])

    @pl.when(r == N_RCV - 2)
    def _():
        scatter(1, xb)

    mid = owners_ref[0] + owners_ref[1] + owners_ref[2] - (N_RCV - 1)
    is_me = jnp.where(mid == r, 1.0, 0.0).astype(jnp.float32)
    is_sib = jnp.where(mid == sib, 1.0, 0.0).astype(jnp.float32)

    def pick(i, carry):
        rows = pl.ds(pl.multiple_of(i * 128, 128), 128)
        mine = own[core, rows, :].astype(jnp.float32) * is_me
        other = xb[rows, :].astype(jnp.float32) * is_sib
        ms[rows, :] = (mine + other).astype(jnp.bfloat16)
        return carry

    lax.fori_loop(0, FREQ // 128, pick, 0)

    for h in range(MIDS):
        for d in (4, 3, 5, 2, 6, 1, 7):
            pltpu.make_async_remote_copy(
                src_ref=ms.at[rows_of(lax.rem(y + d, N_Y) * GROUP + h * HALF, HALF), :],
                dst_ref=mr.at[h, (d - 1) * HALF:d * HALF, :],
                send_sem=mid_s.at[h], recv_sem=mid_r.at[h],
                device_id={"rcv": row_dev(d)}, device_id_type=MESH).start()

    half = LAGS // 2

    def steer(i, carry):
        rows = pl.ds(pl.multiple_of(i * 16, 16), 16)
        low = pl.ds(pl.multiple_of(FREQ + i * 16, 16), 16)
        a = rec[0, rows, :].astype(jnp.float32) * gain
        b = rec[1, rows, :].astype(jnp.float32) * gain
        for l in range(half):
            c = jnp.broadcast_to(tab_ref[rows, l:l + 1], (16, CHAN))
            t = jnp.broadcast_to(tab_ref[rows, half + l:half + l + 1], (16, CHAN))
            ac, bt, at, bc = a * c, b * t, a * t, b * c
            near = slice(l * CHAN, (l + 1) * CHAN)
            far = slice((LAGS - 1 - l) * CHAN, (LAGS - l) * CHAN)
            st[rows, near] = (ac - bt).astype(jnp.bfloat16)
            st[rows, far] = (ac + bt).astype(jnp.bfloat16)
            st[low, near] = (at + bc).astype(jnp.bfloat16)
            st[low, far] = (bc - at).astype(jnp.bfloat16)
        return carry

    load_tab.wait()
    lax.fori_loop(0, FREQ // 16, steer, 0)

    def wait_rows(ref, sem):
        pltpu.make_async_copy(ref, ref, sem).wait()

    def column_send(blk):
        for z2 in range(N_ZH):
            @pl.when(zh != z2)
            def _():
                pltpu.make_async_remote_copy(
                    src_ref=pb.at[blk, my_rows, :], dst_ref=pb.at[blk, my_rows, :],
                    send_sem=z_s.at[blk], recv_sem=z_r.at[blk],
                    device_id={"rcv": (z2 * N_Y + y) * 2 + core}, device_id_type=MESH).start()

    def mid_copy(h, d):
        return pltpu.make_async_remote_copy(
            src_ref=mp.at[h], dst_ref=mz.at[h, d - 1],
            send_sem=mz_s.at[h, d - 1], recv_sem=mz_r.at[h, d - 1],
            device_id={"rcv": column_dev(d)}, device_id_type=MESH)

    def mid_row(h):
        wait_rows(mr.at[h], mid_r.at[h])
        acc = ms[rows_of(y * GROUP + h * HALF, HALF), :]
        for d in range(N_Y - 1):
            acc = acc + mr[h, d * HALF:(d + 1) * HALF, :]
        mp[h] = acc
        for z2 in range(N_ZH):
            @pl.when((zh > 0) & (zh < z2))
            def _():
                pl.semaphore_wait(ready.at[z2], 1)

            @pl.when(zh != z2)
            def _():
                mid_copy(h, lax.rem(z2 - zh + N_ZH, N_ZH)).start()

    def mid_column(h):
        acc = mp[h]
        for d in range(1, N_ZH):
            mid_copy(h, d).wait_recv()
            acc = acc + mz[h, d - 1]
        pb[2, rows_of(base + y * GROUP + h * HALF, HALF), :] = acc

    def ring_at(offset):
        return lax.rem(y + N_Y + offset, N_Y)

    def ring_rows(part_set, offset, way, j):
        _, low, size, _ = part_set
        start = base + ring_at(offset) * GROUP + low
        if j < 3:
            return rows_of(start, size)
        return rows_of(start + way * (size // 2), size // 2)

    def ring_copy(part_set, way, j):
        blk, _, _, at = part_set
        sign = -1 if way else 1
        rows = ring_rows(part_set, 0 if j < 2 else -2 * sign, way, j)
        return pltpu.make_async_remote_copy(
            src_ref=pb.at[blk, rows, :], dst_ref=pb.at[blk, rows, :],
            send_sem=y_s.at[at, way, j], recv_sem=y_r.at[at, way, j],
            device_id={"rcv": row_dev((2, 1, 1, 2)[j] * sign)}, device_id_type=MESH)

    def to_sibling(blk, rows):
        pltpu.make_async_remote_copy(
            src_ref=pb.at[blk, rows, :], dst_ref=pb.at[blk, rows, :],
            send_sem=d_s.at[blk], recv_sem=d_r.at[blk],
            device_id={"rcv": sib}, device_id_type=MESH).start()

    def ring_recv(part_set, j):
        for way in range(2):
            sign = -1 if way else 1
            ring_copy(part_set, way, j).wait_recv()
            if j == 0:
                ring_copy(part_set, way, 2).start()
                ring_copy(part_set, way, 3).start()
        for way in range(2):
            sign = -1 if way else 1
            if part_set[0] not in WHOLE:
                to_sibling(part_set[0], ring_rows(part_set, -(2, 1, 3, 4)[j] * sign, way, j))

    def ring_start(part_set):
        for j in range(2):
            for way in range(2):
                ring_copy(part_set, way, j).start()
        if part_set[0] not in WHOLE:
            to_sibling(part_set[0], ring_rows(part_set, 0, 0, 0))

    def correlate(blk):
        def product(rows, cols):
            return lax.dot_general(
                pb[blk, rows, :], st[rows, cols], (((0,), (0,)), ((), ())),
                preferred_element_type=jnp.float32)

        quarters = [slice(n * 256, (n + 1) * 256) for n in range(4)]
        for cols in quarters:
            acc[:, cols] = product(pl.ds(pl.multiple_of(base, FREQ), FREQ), cols)
        wait_rows(pb.at[blk, pl.ds(0, FREQ), :], d_r.at[blk])
        for half_span in range(SPANS):
            for n in range(4 // SPANS):
                cols = quarters[half_span * (4 // SPANS) + n]
                both = acc[:, cols] + product(pl.ds(pl.multiple_of(FREQ - base, FREQ), FREQ), cols)
                part[blk, half_span, :, n * 256:(n + 1) * 256] = both.astype(jnp.bfloat16)
            for d in (4, 5, 3, 6, 2, 1, 7):
                s2 = shot(d)
                pltpu.make_async_remote_copy(
                    src_ref=part.at[blk, half_span, pl.ds(pl.multiple_of(s2 * ROWS, ROWS), ROWS), :],
                    dst_ref=rb.at[blk, half_span, (d - 1) * ROWS:d * ROWS, :],
                    send_sem=rs_s.at[blk, half_span], recv_sem=rs_r.at[blk, half_span],
                    device_id={"shot": s2}, device_id_type=MESH).start()

    def stack(blk):
        mine = pl.ds(pl.multiple_of(s * ROWS, ROWS), ROWS)
        for l in range(LAGS):
            half_span, n = l // (LAGS // SPANS), l % (LAGS // SPANS)
            if n == 0:
                wait_rows(rb.at[blk, half_span], rs_r.at[blk, half_span])
            cols = slice(n * CHAN, (n + 1) * CHAN)
            total = part[blk, half_span, mine, cols].astype(jnp.float32)
            for d in range(SHOTS - 1):
                total = total + rb[blk, half_span, d * ROWS:(d + 1) * ROWS, cols].astype(jnp.float32)
            res[blk, :, l, :] = total

    sets = [(0, 0, GROUP, 0), (1, 0, GROUP, 1)]
    sets = sets + [(2, h * HALF, HALF, 2 + h) for h in range(MIDS)]

    for blk, root in ((0, 0), (1, CHIPS - 1)):
        @pl.when(zh == root // N_Y)
        def _():
            @pl.when(y != root % N_Y)
            def _():
                wait_rows(pb.at[blk, my_rows, :], scat_r.at[blk])
            if blk == 0:
                ring_start(sets[0])
                for z2 in range(1, N_ZH):
                    pl.semaphore_wait(ready.at[z2], 1)
            column_send(blk)

    for h in range(MIDS):
        mid_row(h)


    for blk, root in ((0, 0), (1, CHIPS - 1)):
        @pl.when(zh != root // N_Y)
        def _():
            wait_rows(pb.at[blk, my_rows, :], z_r.at[blk])
            if blk == 0:
                ring_start(sets[0])
        if blk == 1:
            ring_start(sets[1])
    ring_recv(sets[0], 0)
    for h in range(MIDS):
        mid_column(h)
        ring_start(sets[2 + h])
    ring_recv(sets[1], 0)
    ring_recv(sets[2], 0)

    def ring_rest(blk):
        for part_set in sets:
            if part_set[0] == blk:
                for j in range(1, 4):
                    ring_recv(part_set, j)
        if blk in WHOLE:
            to_sibling(blk, rows_of(base, FREQ))

    ring_rest(0)
    ring_rest(1)
    correlate(0)
    ring_rest(2)
    correlate(1)
    correlate(2)
    swap.wait_send()
    for h in range(MIDS):
        wait_rows(mr.at[h], mid_s.at[h])
        for d in range(1, N_ZH):
            mid_copy(h, d).wait_send()
    for blk, root in ((0, 0), (1, CHIPS - 1)):
        @pl.when(q == root)
        def _():
            wait_rows(pb.at[blk, pl.ds(0, FREQ - GROUP), :], scat_s.at[blk])

        @pl.when(zh == root // N_Y)
        def _():
            wait_rows(pb.at[blk, pl.ds(0, (N_ZH - 1) * GROUP), :], z_s.at[blk])
    for part_set in sets:
        for j in range(4):
            for way in range(2):
                ring_copy(part_set, way, j).wait_send()
    for blk in range(BLOCKS):
        wait_rows(pb.at[blk, pl.ds(0, FREQ), :], d_s.at[blk])

    for blk in range(BLOCKS):
        stack(blk)

    for b in range(BLOCKS):
        owner = jnp.full((ROWS, LAGS, CHAN), owners_ref[b], jnp.int32)
        out_ref[b] = jnp.where(owner == 0, res[0], jnp.where(owner == N_RCV - 1, res[1], res[2]))

    for blk in range(BLOCKS):
        for half_span in range(SPANS):
            wait_rows(rb.at[blk, half_span], rs_s.at[blk, half_span])


def on_device(records, live_mask, owners):
    bf16, f32 = jnp.bfloat16, jnp.float32
    dma = pltpu.SemaphoreType.DMA
    return pl.pallas_call(
        kernel,
        out_shape=pltpu.VMEM((BLOCKS, ROWS, LAGS, CHAN), f32),
        in_specs=[
            pl.BlockSpec(memory_space=pltpu.SMEM),
            pl.BlockSpec(memory_space=pltpu.HBM),
            pl.BlockSpec(memory_space=pltpu.HBM),
            pl.BlockSpec(memory_space=pltpu.HBM),
        ],
        out_specs=pl.BlockSpec(memory_space=pltpu.VMEM),
        scratch_shapes=[
            pltpu.VMEM((1, CHAN), jnp.int32),
            pltpu.VMEM((FREQ, LAGS), f32),
            pltpu.VMEM((2, FREQ, CHAN), bf16),
            pltpu.VMEM((2, FREQ, CHAN), bf16),
            pltpu.VMEM((FREQ, CHAN), bf16),
            pltpu.VMEM((FREQ, CHAN), bf16),
            pltpu.VMEM((MIDS, (N_Y - 1) * HALF, CHAN), bf16),
            pltpu.VMEM((MIDS, HALF, CHAN), bf16),
            pltpu.VMEM((MIDS, N_ZH - 1, HALF, CHAN), bf16),
            pltpu.VMEM((BLOCKS, 2 * FREQ, CHAN), bf16),
            pltpu.VMEM((2 * FREQ, WIDE), bf16),
            pltpu.VMEM((BLOCKS, SPANS, CHAN, SPAN), bf16),
            pltpu.VMEM((BLOCKS, SPANS, (SHOTS - 1) * ROWS, SPAN), bf16),
            pltpu.VMEM((CHAN, WIDE), f32),
            pltpu.VMEM((BLOCKS, ROWS, LAGS, CHAN), f32),
            dma, dma, dma, dma, dma, dma((2,)), dma((2,)), dma((2,)), dma((2,)),
            pltpu.SemaphoreType.REGULAR((N_ZH,)), dma((2, N_ZH - 1)), dma((2, N_ZH - 1)), dma((2,)), dma((2,)),
            dma((4, 2, 4)), dma((4, 2, 4)),
            dma((BLOCKS,)), dma((BLOCKS,)), dma((BLOCKS, 2)), dma((BLOCKS, 2)),
        ],
        cost_estimate=pl.CostEstimate(flops=1_700_000_000, bytes_accessed=1_500_000, transcendentals=0),
        compiler_params=pltpu.CompilerParams(
            collective_id=0, has_side_effects=True, vmem_limit_bytes=62 * 2**20),
    )(owners, live_mask, jnp.asarray(lag_tables()), records.reshape(2, FREQ, CHAN))


def solution(mesh):
    in_specs = (P(None, "shot", None, "rcv"), P("shot", "rcv"), P())
    out_specs = P(None, "shot", None, "rcv")
    return jax.shard_map(
        on_device, mesh=mesh, in_specs=in_specs, out_specs=out_specs, check_vma=False
    )
```

```python
import functools
import math

import jax
import jax.numpy as jnp
import numpy as np
from jax import lax
from jax.experimental import pallas as pl
from jax.experimental.pallas import tpu as pltpu
from jax.sharding import PartitionSpec as P

FREQ = 1024
CHAN = 128
BLOCKS = 3
LAGS = 8
STRIDE = 16
N_ZH = 4
N_Y = 8
CHIPS = N_ZH * N_Y
N_RCV = 2 * CHIPS
SHOTS = 8
GROUP = FREQ // N_Y
MIDS = 1
WHOLE = (0, 1, 2)
HALF = GROUP // MIDS
ROWS = CHAN // SHOTS
WIDE = LAGS * CHAN
SPANS = 2
SPAN = WIDE // SPANS
MESH = pl.DeviceIdType.MESH


def lag_tables():
    f32 = np.float32
    freq_index = np.arange(FREQ, dtype=f32)
    lag_index = np.arange(LAGS, dtype=f32)
    shifts = (lag_index - f32(LAGS // 2)) * f32(STRIDE) + f32(STRIDE // 2)
    taper = f32(0.54) + f32(0.46) * np.cos(f32(2.0 * math.pi) * (lag_index + f32(0.5)) / f32(LAGS) - f32(math.pi))
    phases = f32(math.pi) * freq_index[:, None] * shifts[None, :] / f32(FREQ)
    weights = taper[None, :] / np.sqrt(f32(SHOTS * FREQ))
    half = LAGS // 2
    cos_table = (np.cos(phases) * weights)[:, :half]
    sin_table = (np.sin(phases) * weights)[:, :half]
    return np.concatenate([cos_table, sin_table], axis=1).astype(f32)


def kernel(
    owners_ref, mask_hbm, tab_hbm, rec_hbm, out_ref,
    mask_ref, tab_ref, rec, own, xb, ms, mr, mp, mz, pb, st, part, rb, acc, res,
    mask_sem, tab_sem, load_sem, sib_s, sib_r, scat_s, scat_r, mid_s, mid_r,
    ready, mz_s, mz_r, z_s, z_r, y_s, y_r, d_s, d_r, rs_s, rs_r,
):
    r = lax.axis_index("rcv")
    s = lax.axis_index("shot")
    q = lax.div(r, 2)
    core = lax.rem(r, 2)
    zh = lax.div(q, N_Y)
    y = lax.rem(q, N_Y)
    sib = r + 1 - 2 * core

    def row_dev(d):
        return (zh * N_Y + lax.rem(y + d + N_Y, N_Y)) * 2 + core

    def column_dev(d):
        return (lax.rem(zh + d, N_ZH) * N_Y + y) * 2 + core

    def row_z(z2):
        return (z2 * N_Y + y) * 2 + core

    def shot(d):
        return lax.rem(s + d, SHOTS)

    barrier = pltpu.get_barrier_semaphore()

    def greet(dev):
        pl.semaphore_signal(barrier, inc=1, device_id=dev, device_id_type=MESH)

    load = pltpu.make_async_copy(rec_hbm, rec, load_sem)
    load.start()
    load_mask = pltpu.make_async_copy(mask_hbm, mask_ref, mask_sem)
    load_mask.start()
    load_tab = pltpu.make_async_copy(tab_hbm, tab_ref, tab_sem)
    load_tab.start()
    for d in range(N_Y - 1, 0, -1):
        greet({"rcv": row_dev(d)})
    for z2 in range(1, N_ZH):
        @pl.when(zh < z2)
        def _():
            greet({"rcv": row_z(z2)})
    greet({"rcv": sib})
    for d in range(1, SHOTS):
        greet({"shot": shot(d)})

    load.wait()

    def add_power(i, acc):
        rows = pl.ds(pl.multiple_of(i * 64, 64), 64)
        for p in range(2):
            v = rec[p, rows, :].astype(jnp.float32)
            v = v * v
            for j in range(8):
                acc = acc + v[8 * j:8 * j + 8]
        return acc

    total = lax.fori_loop(0, FREQ // 64, add_power, jnp.zeros((8, CHAN), jnp.float32))
    power = jnp.sum(total, axis=0, keepdims=True) * (1.0 / (2 * FREQ))
    load_mask.wait()
    gain = mask_ref[...].astype(jnp.float32) / jnp.sqrt(power + 1e-06)

    def whiten_part(p):
        def body(i, carry):
            rows = pl.ds(pl.multiple_of(i * 128, 128), 128)
            own[p, rows, :] = (rec[p, rows, :].astype(jnp.float32) * gain).astype(jnp.bfloat16)
            return carry
        lax.fori_loop(0, FREQ // 128, body, 0)

    whiten_part(1 - core)
    pl.semaphore_wait(barrier, N_Y - 1 + zh + 1 + SHOTS - 1)
    swap = pltpu.make_async_remote_copy(
        src_ref=own.at[1 - core], dst_ref=xb, send_sem=sib_s, recv_sem=sib_r,
        device_id={"rcv": sib}, device_id_type=MESH)
    swap.start()
    for z2 in range(N_ZH - 1):
        @pl.when(zh > z2)
        def _():
            pl.semaphore_signal(ready.at[zh], inc=1, device_id={"rcv": row_z(z2)}, device_id_type=MESH)

    whiten_part(core)
    swap.wait_recv()

    base = core * FREQ

    def rows_of(start, size):
        return pl.ds(pl.multiple_of(start, 16), size)

    my_rows = rows_of(base + y * GROUP, GROUP)

    def scatter(blk, src):
        for d in range(1, N_Y):
            row = lax.rem(y + d, N_Y) * GROUP
            pltpu.make_async_remote_copy(
                src_ref=src.at[rows_of(row, GROUP), :],
                dst_ref=pb.at[blk, rows_of(base + row, GROUP), :],
                send_sem=scat_s.at[blk], recv_sem=scat_r.at[blk],
                device_id={"rcv": row_dev(d)}, device_id_type=MESH).start()
        pb[blk, my_rows, :] = src[rows_of(y * GROUP, GROUP), :]

    @pl.when(r == 0)
    def _():
        scatter(0, own.at[0])

    @pl.when(r == 1)
    def _():
        scatter(0, xb)

    @pl.when(r == N_RCV - 1)
    def _():
        scatter(1, own.at[1])

    @pl.when(r == N_RCV - 2)
    def _():
        scatter(1, xb)

    mid = owners_ref[0] + owners_ref[1] + owners_ref[2] - (N_RCV - 1)
    is_me = jnp.where(mid == r, 1.0, 0.0).astype(jnp.float32)
    is_sib = jnp.where(mid == sib, 1.0, 0.0).astype(jnp.float32)

    def pick(i, carry):
        rows = pl.ds(pl.multiple_of(i * 128, 128), 128)
        mine = own[core, rows, :].astype(jnp.float32) * is_me
        other = xb[rows, :].astype(jnp.float32) * is_sib
        ms[rows, :] = (mine + other).astype(jnp.bfloat16)
        return carry

    lax.fori_loop(0, FREQ // 128, pick, 0)

    for h in range(MIDS):
        for d in (4, 3, 5, 2, 6, 1, 7):
            pltpu.make_async_remote_copy(
                src_ref=ms.at[rows_of(lax.rem(y + d, N_Y) * GROUP + h * HALF, HALF), :],
                dst_ref=mr.at[h, (d - 1) * HALF:d * HALF, :],
                send_sem=mid_s.at[h], recv_sem=mid_r.at[h],
                device_id={"rcv": row_dev(d)}, device_id_type=MESH).start()

    half = LAGS // 2

    def steer(i, carry):
        rows = pl.ds(pl.multiple_of(i * 16, 16), 16)
        low = pl.ds(pl.multiple_of(FREQ + i * 16, 16), 16)
        a = rec[0, rows, :].astype(jnp.float32) * gain
        b = rec[1, rows, :].astype(jnp.float32) * gain
        for l in range(half):
            c = jnp.broadcast_to(tab_ref[rows, l:l + 1], (16, CHAN))
            t = jnp.broadcast_to(tab_ref[rows, half + l:half + l + 1], (16, CHAN))
            ac, bt, at, bc = a * c, b * t, a * t, b * c
            near = slice(l * CHAN, (l + 1) * CHAN)
            far = slice((LAGS - 1 - l) * CHAN, (LAGS - l) * CHAN)
            st[rows, near] = (ac - bt).astype(jnp.bfloat16)
            st[rows, far] = (ac + bt).astype(jnp.bfloat16)
            st[low, near] = (at + bc).astype(jnp.bfloat16)
            st[low, far] = (bc - at).astype(jnp.bfloat16)
        return carry

    load_tab.wait()
    lax.fori_loop(0, FREQ // 16, steer, 0)

    def wait_rows(ref, sem):
        pltpu.make_async_copy(ref, ref, sem).wait()

    def column_send(blk):
        for z2 in range(N_ZH):
            @pl.when(zh != z2)
            def _():
                pltpu.make_async_remote_copy(
                    src_ref=pb.at[blk, my_rows, :], dst_ref=pb.at[blk, my_rows, :],
                    send_sem=z_s.at[blk], recv_sem=z_r.at[blk],
                    device_id={"rcv": (z2 * N_Y + y) * 2 + core}, device_id_type=MESH).start()

    def mid_copy(h, d):
        return pltpu.make_async_remote_copy(
            src_ref=mp.at[h], dst_ref=mz.at[h, d - 1],
            send_sem=mz_s.at[h, d - 1], recv_sem=mz_r.at[h, d - 1],
            device_id={"rcv": column_dev(d)}, device_id_type=MESH)

    def mid_row(h):
        wait_rows(mr.at[h], mid_r.at[h])
        acc = ms[rows_of(y * GROUP + h * HALF, HALF), :]
        for d in range(N_Y - 1):
            acc = acc + mr[h, d * HALF:(d + 1) * HALF, :]
        mp[h] = acc
        for z2 in range(N_ZH):
            @pl.when((zh > 0) & (zh < z2))
            def _():
                pl.semaphore_wait(ready.at[z2], 1)

            @pl.when(zh != z2)
            def _():
                mid_copy(h, lax.rem(z2 - zh + N_ZH, N_ZH)).start()

    def mid_column(h):
        acc = mp[h]
        for d in range(1, N_ZH):
            mid_copy(h, d).wait_recv()
            acc = acc + mz[h, d - 1]
        pb[2, rows_of(base + y * GROUP + h * HALF, HALF), :] = acc

    def ring_at(offset):
        return lax.rem(y + N_Y + offset, N_Y)

    def ring_rows(part_set, offset, way, j):
        _, low, size, _ = part_set
        start = base + ring_at(offset) * GROUP + low
        if j < 3:
            return rows_of(start, size)
        return rows_of(start + way * (size // 2), size // 2)

    def ring_copy(part_set, way, j):
        blk, _, _, at = part_set
        sign = -1 if way else 1
        rows = ring_rows(part_set, 0 if j < 2 else -2 * sign, way, j)
        return pltpu.make_async_remote_copy(
            src_ref=pb.at[blk, rows, :], dst_ref=pb.at[blk, rows, :],
            send_sem=y_s.at[at, way, j], recv_sem=y_r.at[at, way, j],
            device_id={"rcv": row_dev((2, 1, 1, 2)[j] * sign)}, device_id_type=MESH)

    def to_sibling(blk, rows):
        pltpu.make_async_remote_copy(
            src_ref=pb.at[blk, rows, :], dst_ref=pb.at[blk, rows, :],
            send_sem=d_s.at[blk], recv_sem=d_r.at[blk],
            device_id={"rcv": sib}, device_id_type=MESH).start()

    def ring_recv(part_set, j):
        for way in range(2):
            sign = -1 if way else 1
            ring_copy(part_set, way, j).wait_recv()
            if j == 0:
                ring_copy(part_set, way, 2).start()
                ring_copy(part_set, way, 3).start()
        for way in range(2):
            sign = -1 if way else 1
            if part_set[0] not in WHOLE:
                to_sibling(part_set[0], ring_rows(part_set, -(2, 1, 3, 4)[j] * sign, way, j))

    def ring_start(part_set):
        for j in range(2):
            for way in range(2):
                ring_copy(part_set, way, j).start()
        if part_set[0] not in WHOLE:
            to_sibling(part_set[0], ring_rows(part_set, 0, 0, 0))

    def correlate(blk):
        def product(rows, cols):
            return lax.dot_general(
                pb[blk, rows, :], st[rows, cols], (((0,), (0,)), ((), ())),
                preferred_element_type=jnp.float32)

        quarters = [slice(n * 256, (n + 1) * 256) for n in range(4)]
        for cols in quarters:
            acc[:, cols] = product(pl.ds(pl.multiple_of(base, FREQ), FREQ), cols)
        wait_rows(pb.at[blk, pl.ds(0, FREQ), :], d_r.at[blk])
        for half_span in range(SPANS):
            for n in range(4 // SPANS):
                cols = quarters[half_span * (4 // SPANS) + n]
                both = acc[:, cols] + product(pl.ds(pl.multiple_of(FREQ - base, FREQ), FREQ), cols)
                part[blk, half_span, :, n * 256:(n + 1) * 256] = both.astype(jnp.bfloat16)
            for d in (4, 5, 3, 6, 2, 1, 7):
                s2 = shot(d)
                pltpu.make_async_remote_copy(
                    src_ref=part.at[blk, half_span, pl.ds(pl.multiple_of(s2 * ROWS, ROWS), ROWS), :],
                    dst_ref=rb.at[blk, half_span, (d - 1) * ROWS:d * ROWS, :],
                    send_sem=rs_s.at[blk, half_span], recv_sem=rs_r.at[blk, half_span],
                    device_id={"shot": s2}, device_id_type=MESH).start()

    def stack(blk):
        mine = pl.ds(pl.multiple_of(s * ROWS, ROWS), ROWS)
        for l in range(LAGS):
            half_span, n = l // (LAGS // SPANS), l % (LAGS // SPANS)
            if n == 0:
                wait_rows(rb.at[blk, half_span], rs_r.at[blk, half_span])
            cols = slice(n * CHAN, (n + 1) * CHAN)
            total = part[blk, half_span, mine, cols].astype(jnp.float32)
            for d in range(SHOTS - 1):
                total = total + rb[blk, half_span, d * ROWS:(d + 1) * ROWS, cols].astype(jnp.float32)
            res[blk, :, l, :] = total

    sets = [(0, 0, GROUP, 0), (1, 0, GROUP, 1)]
    sets = sets + [(2, h * HALF, HALF, 2 + h) for h in range(MIDS)]

    for blk, root in ((0, 0), (1, CHIPS - 1)):
        @pl.when(zh == root // N_Y)
        def _():
            @pl.when(y != root % N_Y)
            def _():
                wait_rows(pb.at[blk, my_rows, :], scat_r.at[blk])
            if blk == 0:
                ring_start(sets[0])
                for z2 in range(1, N_ZH):
                    pl.semaphore_wait(ready.at[z2], 1)
            column_send(blk)

    for h in range(MIDS):
        mid_row(h)


    for blk, root in ((0, 0), (1, CHIPS - 1)):
        @pl.when(zh != root // N_Y)
        def _():
            wait_rows(pb.at[blk, my_rows, :], z_r.at[blk])
            if blk == 0:
                ring_start(sets[0])
        if blk == 1:
            ring_start(sets[1])
    ring_recv(sets[0], 0)
    for h in range(MIDS):
        mid_column(h)
        ring_start(sets[2 + h])
    ring_recv(sets[1], 0)
    ring_recv(sets[2], 0)

    def ring_rest(blk):
        for part_set in sets:
            if part_set[0] == blk:
                for j in range(1, 4):
                    ring_recv(part_set, j)
        if blk in WHOLE:
            to_sibling(blk, rows_of(base, FREQ))

    ring_rest(0)
    ring_rest(1)
    correlate(0)
    correlate(1)
    ring_rest(2)
    correlate(2)
    swap.wait_send()
    for h in range(MIDS):
        wait_rows(mr.at[h], mid_s.at[h])
        for d in range(1, N_ZH):
            mid_copy(h, d).wait_send()
    for blk, root in ((0, 0), (1, CHIPS - 1)):
        @pl.when(q == root)
        def _():
            wait_rows(pb.at[blk, pl.ds(0, FREQ - GROUP), :], scat_s.at[blk])

        @pl.when(zh == root // N_Y)
        def _():
            wait_rows(pb.at[blk, pl.ds(0, (N_ZH - 1) * GROUP), :], z_s.at[blk])
    for part_set in sets:
        for j in range(4):
            for way in range(2):
                ring_copy(part_set, way, j).wait_send()
    for blk in range(BLOCKS):
        wait_rows(pb.at[blk, pl.ds(0, FREQ), :], d_s.at[blk])

    for blk in range(BLOCKS):
        stack(blk)

    for b in range(BLOCKS):
        owner = jnp.full((ROWS, LAGS, CHAN), owners_ref[b], jnp.int32)
        out_ref[b] = jnp.where(owner == 0, res[0], jnp.where(owner == N_RCV - 1, res[1], res[2]))

    for blk in range(BLOCKS):
        for half_span in range(SPANS):
            wait_rows(rb.at[blk, half_span], rs_s.at[blk, half_span])


def on_device(records, live_mask, owners):
    bf16, f32 = jnp.bfloat16, jnp.float32
    dma = pltpu.SemaphoreType.DMA
    return pl.pallas_call(
        kernel,
        out_shape=pltpu.VMEM((BLOCKS, ROWS, LAGS, CHAN), f32),
        in_specs=[
            pl.BlockSpec(memory_space=pltpu.SMEM),
            pl.BlockSpec(memory_space=pltpu.HBM),
            pl.BlockSpec(memory_space=pltpu.HBM),
            pl.BlockSpec(memory_space=pltpu.HBM),
        ],
        out_specs=pl.BlockSpec(memory_space=pltpu.VMEM),
        scratch_shapes=[
            pltpu.VMEM((1, CHAN), jnp.int32),
            pltpu.VMEM((FREQ, LAGS), f32),
            pltpu.VMEM((2, FREQ, CHAN), bf16),
            pltpu.VMEM((2, FREQ, CHAN), bf16),
            pltpu.VMEM((FREQ, CHAN), bf16),
            pltpu.VMEM((FREQ, CHAN), bf16),
            pltpu.VMEM((MIDS, (N_Y - 1) * HALF, CHAN), bf16),
            pltpu.VMEM((MIDS, HALF, CHAN), bf16),
            pltpu.VMEM((MIDS, N_ZH - 1, HALF, CHAN), bf16),
            pltpu.VMEM((BLOCKS, 2 * FREQ, CHAN), bf16),
            pltpu.VMEM((2 * FREQ, WIDE), bf16),
            pltpu.VMEM((BLOCKS, SPANS, CHAN, SPAN), bf16),
            pltpu.VMEM((BLOCKS, SPANS, (SHOTS - 1) * ROWS, SPAN), bf16),
            pltpu.VMEM((CHAN, WIDE), f32),
            pltpu.VMEM((BLOCKS, ROWS, LAGS, CHAN), f32),
            dma, dma, dma, dma, dma, dma((2,)), dma((2,)), dma((2,)), dma((2,)),
            pltpu.SemaphoreType.REGULAR((N_ZH,)), dma((2, N_ZH - 1)), dma((2, N_ZH - 1)), dma((2,)), dma((2,)),
            dma((4, 2, 4)), dma((4, 2, 4)),
            dma((BLOCKS,)), dma((BLOCKS,)), dma((BLOCKS, 2)), dma((BLOCKS, 2)),
        ],
        cost_estimate=pl.CostEstimate(flops=1_700_000_000, bytes_accessed=1_500_000, transcendentals=0),
        compiler_params=pltpu.CompilerParams(
            collective_id=0, has_side_effects=True, vmem_limit_bytes=62 * 2**20),
    )(owners, live_mask, jnp.asarray(lag_tables()), records.reshape(2, FREQ, CHAN))


def solution(mesh):
    in_specs = (P(None, "shot", None, "rcv"), P("shot", "rcv"), P())
    out_specs = P(None, "shot", None, "rcv")
    return jax.shard_map(
        on_device, mesh=mesh, in_specs=in_specs, out_specs=out_specs, check_vma=False
    )
```
